128 devices in a mesh: dp: 8 (over z, y_lo), tensor: 16 (over y_hi, x, core).
Axes of the slice: x: 4, y: 4 (y_hi: 2, y_lo: 2; y = y_hi * 2 + y_lo), z: 4, core: 2. Of those that a mesh axis runs over, the one named last changes fastest.
Arguments:
- gate_input: bfloat16 [2048, 26624], P('dp', 'tensor'), parts along dimension 0, may hold values from -6 to 6
- up_input: bfloat16 [2048, 26624], P('dp', 'tensor'), parts along dimension 0, may hold values from -6 to 6
- down_low: int32 [3328, 8192], P('tensor'), may hold values from -34952 to 30583
- down_high: int32 [3328, 8192], P('tensor'), may hold values from -34952 to 30583
- down_scales: bfloat16 [208, 8192], P('tensor'), may hold values from 0.00024414062 to 0.002746582
Outputs:
- mixed: bfloat16 [2048, 8192], P('dp'), parts along dimension 0
The draws below stay inside these ranges and needn't reach their ends.
There are 8 independent parts, one for each index of `dp`. The reference program is written for one: setup_inputs(seed, part) draws one part's arguments, and reference() takes and returns one part's arrays. A program takes and returns all parts, laid end to end along the dimension named above; an argument that names none is the same for every part. Nothing has to cross between parts.
All inputs are finite; a program needn't handle non-finite values.
Results may differ from the reference program's by a relative error of at most 0.0065.
Values may be sent and summed in bfloat16 or wider, within the bound.
No kernel may reach another device: no remote copies, remote signals or barrier semaphores. Data moves between devices by JAX's collectives and lax.ppermute only.
A program may use at most 192 MiB of HBM per device.

```python
import math
import jax
import jax.numpy as jnp
import numpy as np
from jax import lax

D = 8192
FF = 26624
GROUP = 128
ROWS = 256


def with_ends(values, key, smallest, largest):
    dims = values.shape
    spot = [jax.random.randint(jax.random.fold_in(key, axis), (), 0, dims[axis]) for axis in range(len(dims))]
    values = values.at[tuple(spot)].set(smallest)
    longest = dims.index(max(dims))
    spot[longest] = (spot[longest] + 1) % dims[longest]
    return values.at[tuple(spot)].set(largest)


def block_scale(stream_key, shape, pieces, smallest, largest):
    gain, own = 1.0, jax.random.fold_in(stream_key, 6)
    for axis_at, shards_of in pieces:
        heights = jnp.exp(jax.random.uniform(jax.random.fold_in(own, axis_at), (shards_of,), jnp.float32, smallest / len(pieces), largest / len(pieces)))
        gain = gain * jnp.repeat(heights, shape[axis_at] // shards_of).reshape([-1 if axis == axis_at else 1 for axis in range(len(shape))])
    return gain


def noise(own_key, shape, deviation, reach, pieces=(), kind=jnp.bfloat16):
    values = jax.random.normal(own_key, shape, jnp.float32) * deviation
    if len(pieces) > 0:
        values = block_scale(own_key, shape, pieces, -0.22, 0.18) * values
    return jnp.clip(values, min=-reach, max=reach).astype(kind)


def setup_inputs(seed: int = 0, part: int = 0) -> dict:
    key_list = jax.random.split(jax.random.key(seed), 6)
    part_splits = jax.random.split(jax.random.fold_in(key_list[5], part), 6)
    gate_input = noise(part_splits[0], (ROWS, FF), 1.0, 6.0, ((1, 16),))
    up_input = noise(part_splits[1], (ROWS, FF), 1.0, 6.0, ((1, 16),))
    down_low = with_ends(jax.random.randint(key_list[2], (FF // 8, D), -34952, 30584), jax.random.fold_in(key_list[2], 1), -34952, 30583).astype(jnp.int32)
    down_high = with_ends(jax.random.randint(key_list[3], (FF // 8, D), -34952, 30584), jax.random.fold_in(key_list[3], 1), -34952, 30583).astype(jnp.int32)
    down_scales = jnp.clip(jnp.exp(math.log(0.002746582) - 2.4203681 * jax.random.uniform(key_list[4], (FF // GROUP, D), jnp.float32) ** block_scale(key_list[4], (FF // GROUP, D), ((0, 16),), -0.2, 0.2)), 0.00024414062, 0.002746582).astype(jnp.bfloat16)
    return dict(gate_input=gate_input, up_input=up_input, down_low=down_low, down_high=down_high, down_scales=down_scales)


code_offset = 34952

def paley_table():
    elements = [(u, v) for v in range(5) for u in range(5)]
    squares = set()
    for u, v in elements:
        if u != 0 or v != 0:
            squares.add(((u * u + 2 * v * v) % 5, 2 * u * v % 5))
    quad = np.zeros((25, 25))
    for i, first in enumerate(elements):
        for j, second in enumerate(elements):
            diff = ((first[0] - second[0]) % 5, (first[1] - second[1]) % 5)
            if diff != (0, 0):
                quad[i, j] = 1.0 if diff in squares else -1.0
    core = np.zeros((26, 26))
    core[0, 1:] = 1.0
    core[1:, 0] = 1.0
    core[1:, 1:] = quad
    return np.kron(core, np.array([[1.0, 1.0], [1.0, -1.0]])) + np.kron(np.eye(26), np.array([[1.0, -1.0], [-1.0, -1.0]]))

def sylvester(order):
    table = np.ones((1, 1))
    while table.shape[0] < order:
        table = np.kron(np.array([[1.0, 1.0], [1.0, -1.0]]), table)
    return table

def dequant(low_words, high_words, scales):
    shifts = 4 * jnp.arange(4, dtype=jnp.int32)
    low = (low_words + code_offset)[:, None, :] >> shifts[None, :, None] & 15
    high = (high_words + code_offset)[:, None, :] >> shifts[None, :, None] & 15
    nibbles = jnp.concatenate([low, high], axis=1)
    count = low_words.shape[0] * 8
    width = low_words.shape[1]
    codes = nibbles.reshape(count, width).astype(jnp.float32) - 8.0
    groups = scales.shape[0]
    scaled = codes.reshape(groups, count // groups, width) * scales.astype(jnp.float32)[:, None, :]
    return scaled.reshape(count, width).astype(jnp.bfloat16)

def reference(gate_input, up_input, down_low, down_high, down_scales):
    count = gate_input.shape[0]
    hidden = (jax.nn.silu(gate_input.astype(jnp.float32)) * up_input.astype(jnp.float32)).astype(jnp.bfloat16)
    outer = jnp.asarray(sylvester(FF // 52), jnp.float32)
    small = jnp.asarray(paley_table(), jnp.float32)
    spread = hidden.astype(jnp.float32).reshape(count, FF // 52, 52)
    spread = jnp.einsum('rba,ae->rbe', spread, small, precision=lax.Precision.HIGHEST)
    spread = jnp.einsum('rbe,bc->rce', spread, outer, precision=lax.Precision.HIGHEST)
    rotated = (spread.reshape(count, FF) * (1.0 / math.sqrt(FF))).astype(jnp.bfloat16)
    hidden_blocks = FF // GROUP
    rot_pieces = rotated.reshape(count, hidden_blocks, GROUP).transpose(1, 0, 2)
    low_words = down_low.reshape(hidden_blocks, GROUP // 8, D)
    high_words = down_high.reshape(hidden_blocks, GROUP // 8, D)
    down_parts = down_scales.reshape(hidden_blocks, 1, D)

    def outer_step(total, item):
        piece, lword, hword, dpart = item
        return (total + jnp.dot(piece, dequant(lword, hword, dpart), preferred_element_type=jnp.float32), None)
    total, _ = lax.scan(outer_step, jnp.zeros((count, D), jnp.float32), (rot_pieces, low_words, high_words, down_parts))
    return total.astype(jnp.bfloat16)
```

```python
import functools
import math

import jax
import jax.numpy as jnp
import numpy as np
from jax import lax
from jax.experimental import pallas as pl
from jax.experimental.pallas import tpu as pltpu
from jax.sharding import PartitionSpec as P

FF = 26624
GROUP = 128
CODE_FLIP = 0x8888
VMEM_LIMIT = 48 * 1024 * 1024


def paley_table():
    elements = [(u, v) for v in range(5) for u in range(5)]
    squares = set()
    for u, v in elements:
        if u != 0 or v != 0:
            squares.add(((u * u + 2 * v * v) % 5, 2 * u * v % 5))
    quad = np.zeros((25, 25))
    for i, first in enumerate(elements):
        for j, second in enumerate(elements):
            diff = ((first[0] - second[0]) % 5, (first[1] - second[1]) % 5)
            if diff != (0, 0):
                quad[i, j] = 1.0 if diff in squares else -1.0
    core = np.zeros((26, 26))
    core[0, 1:] = 1.0
    core[1:, 0] = 1.0
    core[1:, 1:] = quad
    return np.kron(core, np.array([[1.0, 1.0], [1.0, -1.0]])) + np.kron(
        np.eye(26), np.array([[1.0, -1.0], [-1.0, -1.0]])
    )


def sylvester(order):
    table = np.ones((1, 1))
    while table.shape[0] < order:
        table = np.kron(np.array([[1.0, 1.0], [1.0, -1.0]]), table)
    return table


def local_table(local_ff):
    table = np.kron(sylvester(local_ff // 52), paley_table())
    order = np.arange(local_ff).reshape(-1, GROUP // 8, 8).transpose(0, 2, 1).reshape(-1)
    return jnp.asarray(table[:, order], jnp.bfloat16)


def rotate_body(hidden_ref, table_ref, out_ref):
    shards, rows, depth = hidden_ref.shape
    flat = hidden_ref[...].reshape(shards * rows, depth)
    turned = jnp.dot(flat, table_ref[...], preferred_element_type=jnp.float32)
    parts = [turned[rows * s : rows * (s + 1)] for s in range(shards)]
    step = 1
    while step < shards:
        parts = [
            parts[s] + parts[s + step] if s & step == 0 else parts[s - step] - parts[s]
            for s in range(shards)
        ]
        step *= 2
    for s in range(shards):
        out_ref[s] = (parts[s] * (1.0 / math.sqrt(FF))).astype(jnp.bfloat16)


def rotate(hidden, table):
    shards, rows, depth = hidden.shape
    tile = GROUP
    return pl.pallas_call(
        rotate_body,
        grid=(depth // tile,),
        in_specs=[
            pl.BlockSpec((shards, rows, depth), lambda j: (0, 0, 0)),
            pl.BlockSpec((depth, tile), lambda j: (0, j)),
        ],
        out_specs=pl.BlockSpec((shards, rows, tile), lambda j: (0, 0, j)),
        out_shape=jax.ShapeDtypeStruct(hidden.shape, jnp.bfloat16),
        compiler_params=pltpu.CompilerParams(vmem_limit_bytes=VMEM_LIMIT),
        cost_estimate=pl.CostEstimate(
            flops=2 * shards * rows * depth * depth,
            bytes_accessed=2 * depth * depth + 4 * shards * rows * depth,
            transcendentals=0,
        ),
        name="rotate",
    )(hidden, table)


def dequant_body(low_ref, high_ref, scale_ref, out_ref):
    groups, words, width = low_ref.shape
    for g in range(groups):
        scale = jnp.broadcast_to(scale_ref[g], (words, width))
        for half, ref in enumerate((low_ref, high_ref)):
            nibbles = (ref[g] + 34952) ^ CODE_FLIP
            for k in range(4):
                code = (nibbles << (28 - 4 * k)) >> 28
                out_ref[g, 4 * half + k] = code.astype(jnp.bfloat16) * scale


def dequant(low, high, scales):
    groups, words, width = low.shape
    tile = 512
    return pl.pallas_call(
        dequant_body,
        grid=(width // tile,),
        in_specs=[
            pl.BlockSpec((groups, words, tile), lambda j: (0, 0, j)),
            pl.BlockSpec((groups, words, tile), lambda j: (0, 0, j)),
            pl.BlockSpec((groups, 1, tile), lambda j: (0, 0, j)),
        ],
        out_specs=pl.BlockSpec((groups, 8, words, tile), lambda j: (0, 0, 0, j)),
        out_shape=jax.ShapeDtypeStruct((groups, 8, words, width), jnp.bfloat16),
        compiler_params=pltpu.CompilerParams(vmem_limit_bytes=VMEM_LIMIT),
        cost_estimate=pl.CostEstimate(
            flops=groups * words * 8 * width * 8,
            bytes_accessed=groups * words * width * 24,
            transcendentals=0,
        ),
        name="dequant",
    )(low, high, scales)


def project_body(core_ref, rot_ref, weight_ref, keep_ref, send_ref):
    core = core_ref[0]
    groups, planes, words, tile = weight_ref.shape
    pairs, _, rows, depth = rot_ref.shape
    weight = weight_ref[...].reshape(depth, tile)
    for out_ref, which in ((send_ref, 1 - core), (keep_ref, core)):
        lhs = rot_ref[:, pl.ds(which, 1)].reshape(pairs * rows, depth)
        term = jnp.dot(lhs, weight, preferred_element_type=jnp.float32)
        out_ref[...] = term.astype(jnp.bfloat16).reshape(pairs, rows, tile)


def project(core, rot, weight, first, width):
    pairs, two, rows, depth = rot.shape
    groups, planes, words, _ = weight.shape
    tile = 512
    start = first // tile
    shape = jax.ShapeDtypeStruct((pairs, rows, width), jnp.bfloat16)
    return pl.pallas_call(
        project_body,
        grid_spec=pltpu.PrefetchScalarGridSpec(
            num_scalar_prefetch=1,
            grid=(width // tile,),
            in_specs=[
                pl.BlockSpec((pairs, two, rows, depth), lambda j, c: (0, 0, 0, 0)),
                pl.BlockSpec((groups, planes, words, tile), lambda j, c: (0, 0, 0, j + start)),
            ],
            out_specs=[
                pl.BlockSpec((pairs, rows, tile), lambda j, c: (0, 0, j)),
                pl.BlockSpec((pairs, rows, tile), lambda j, c: (0, 0, j)),
            ],
        ),
        out_shape=[shape, shape],
        compiler_params=pltpu.CompilerParams(vmem_limit_bytes=VMEM_LIMIT),
        cost_estimate=pl.CostEstimate(
            flops=4 * pairs * rows * depth * width,
            bytes_accessed=2 * depth * width + 8 * pairs * rows * width,
            transcendentals=0,
        ),
        name="project",
    )(core, rot, weight)


def local(gate_input, up_input, down_low, down_high, down_scales):
    shards = lax.axis_size("tensor")
    position = lax.axis_index("tensor")
    core = position % 2
    total_rows, local_ff = gate_input.shape
    rows = total_rows // shards
    pairs = shards // 2
    groups = local_ff // GROUP
    width = down_low.shape[1]
    same_core = [[2 * i + c for i in range(pairs)] for c in range(2)]
    other_core = [(i, i ^ 1) for i in range(shards)]

    hidden = (jax.nn.silu(gate_input.astype(jnp.float32)) * up_input.astype(jnp.float32)).astype(jnp.bfloat16)
    mine = lax.all_to_all(hidden.reshape(shards, rows, local_ff), "tensor", 0, 0)
    turned = rotate(mine, local_table(local_ff))
    rot = lax.all_to_all(turned, "tensor", 0, 0).reshape(pairs, 2, rows, local_ff)

    weight = dequant(
        down_low.reshape(groups, GROUP // 8, width),
        down_high.reshape(groups, GROUP // 8, width),
        down_scales.reshape(groups, 1, width),
    )

    core_arg = core.astype(jnp.int32).reshape(1)
    chunks = 2
    part = width // chunks
    sums = []
    for j in range(chunks):
        keep, send = project(core_arg, rot, weight, j * part, part)
        got = lax.ppermute(send, "tensor", other_core)
        chip = (keep.astype(jnp.float32) + got.astype(jnp.float32)).astype(jnp.bfloat16)
        pieces = lax.all_to_all(chip, "tensor", 0, 0, axis_index_groups=same_core)
        sums.append(jnp.sum(pieces.astype(jnp.float32), axis=0).astype(jnp.bfloat16))
    outs = []
    for j in range(chunks):
        spread = jnp.broadcast_to(sums[j][None], (pairs, rows, part))
        own = lax.all_to_all(spread, "tensor", 0, 0, axis_index_groups=same_core)
        theirs = lax.ppermute(own, "tensor", other_core)
        first = jnp.where(core == 0, own, theirs)
        second = jnp.where(core == 0, theirs, own)
        outs.append(jnp.stack([first, second], axis=1).reshape(total_rows, part))
    return jnp.concatenate(outs, axis=1)


def solution(mesh):
    placed = (
        P("dp", "tensor"),
        P("dp", "tensor"),
        P("tensor", None),
        P("tensor", None),
        P("tensor", None),
    )
    return jax.shard_map(local, mesh=mesh, in_specs=placed, out_specs=P("dp", None), check_vma=False)
```

```python
import functools
import math

import jax
import jax.numpy as jnp
import numpy as np
from jax import lax
from jax.experimental import pallas as pl
from jax.experimental.pallas import tpu as pltpu
from jax.sharding import PartitionSpec as P

FF = 26624
GROUP = 128
CODE_FLIP = 0x8888
VMEM_LIMIT = 48 * 1024 * 1024


def paley_table():
    elements = [(u, v) for v in range(5) for u in range(5)]
    squares = set()
    for u, v in elements:
        if u != 0 or v != 0:
            squares.add(((u * u + 2 * v * v) % 5, 2 * u * v % 5))
    quad = np.zeros((25, 25))
    for i, first in enumerate(elements):
        for j, second in enumerate(elements):
            diff = ((first[0] - second[0]) % 5, (first[1] - second[1]) % 5)
            if diff != (0, 0):
                quad[i, j] = 1.0 if diff in squares else -1.0
    core = np.zeros((26, 26))
    core[0, 1:] = 1.0
    core[1:, 0] = 1.0
    core[1:, 1:] = quad
    return np.kron(core, np.array([[1.0, 1.0], [1.0, -1.0]])) + np.kron(
        np.eye(26), np.array([[1.0, -1.0], [-1.0, -1.0]])
    )


def sylvester(order):
    table = np.ones((1, 1))
    while table.shape[0] < order:
        table = np.kron(np.array([[1.0, 1.0], [1.0, -1.0]]), table)
    return table


def local_table(local_ff):
    table = np.kron(sylvester(local_ff // 52), paley_table())
    order = np.arange(local_ff).reshape(-1, GROUP // 8, 8).transpose(0, 2, 1).reshape(-1)
    return jnp.asarray(table[:, order], jnp.bfloat16)


def rotate_body(hidden_ref, table_ref, out_ref, turned_ref):
    shards, rows, depth = hidden_ref.shape
    flat = hidden_ref[...].reshape(shards * rows, depth)
    turned_ref[...] = jnp.dot(flat, table_ref[...], preferred_element_type=jnp.float32)
    width = table_ref.shape[1]
    for first in range(0, width, GROUP):
        cols = slice(first, first + GROUP)
        parts = [turned_ref[rows * s : rows * (s + 1), cols] for s in range(shards)]
        step = 1
        while step < shards:
            parts = [
                parts[s] + parts[s + step] if s & step == 0 else parts[s - step] - parts[s]
                for s in range(shards)
            ]
            step *= 2
        for s in range(shards):
            out_ref[s, :, cols] = (parts[s] * (1.0 / math.sqrt(FF))).astype(jnp.bfloat16)


def rotate(hidden, table):
    shards, rows, depth = hidden.shape
    tile = 896
    return pl.pallas_call(
        rotate_body,
        grid=(pl.cdiv(depth, tile),),
        in_specs=[
            pl.BlockSpec((shards, rows, depth), lambda j: (0, 0, 0)),
            pl.BlockSpec((depth, tile), lambda j: (0, j)),
        ],
        out_specs=pl.BlockSpec((shards, rows, tile), lambda j: (0, 0, j)),
        out_shape=jax.ShapeDtypeStruct(hidden.shape, jnp.bfloat16),
        scratch_shapes=[pltpu.VMEM((shards * rows, tile), jnp.float32)],
        compiler_params=pltpu.CompilerParams(vmem_limit_bytes=VMEM_LIMIT),
        cost_estimate=pl.CostEstimate(
            flops=2 * shards * rows * depth * depth,
            bytes_accessed=2 * depth * depth + 4 * shards * rows * depth,
            transcendentals=0,
        ),
        name="rotate",
    )(hidden, table)


def dequant_body(low_ref, high_ref, scale_ref, out_ref):
    groups, words, width = low_ref.shape
    for g in range(groups):
        scale = jnp.broadcast_to(scale_ref[g], (words, width))
        for half, ref in enumerate((low_ref, high_ref)):
            nibbles = (ref[g] + 34952) ^ CODE_FLIP
            for k in range(4):
                code = (nibbles << (28 - 4 * k)) >> 28
                out_ref[g, 4 * half + k] = code.astype(jnp.bfloat16) * scale


def dequant(low, high, scales):
    groups, words, width = low.shape
    tile = 512
    return pl.pallas_call(
        dequant_body,
        grid=(width // tile,),
        in_specs=[
            pl.BlockSpec((groups, words, tile), lambda j: (0, 0, j)),
            pl.BlockSpec((groups, words, tile), lambda j: (0, 0, j)),
            pl.BlockSpec((groups, 1, tile), lambda j: (0, 0, j)),
        ],
        out_specs=pl.BlockSpec((groups, 8, words, tile), lambda j: (0, 0, 0, j)),
        out_shape=jax.ShapeDtypeStruct((groups, 8, words, width), jnp.bfloat16),
        compiler_params=pltpu.CompilerParams(vmem_limit_bytes=VMEM_LIMIT),
        cost_estimate=pl.CostEstimate(
            flops=groups * words * 8 * width * 8,
            bytes_accessed=groups * words * width * 24,
            transcendentals=0,
        ),
        name="dequant",
    )(low, high, scales)


def project_body(order, place_ref, rot_ref, weight_ref, keep_ref, send_ref, lhs_ref):
    groups, planes, words, tile = weight_ref.shape
    shards, rows, depth = rot_ref.shape
    place = place_ref[0]

    @pl.when(pl.program_id(0) == 0)
    def _():
        for at, block in enumerate(order):
            lhs_ref[rows * at : rows * (at + 1)] = rot_ref[jnp.bitwise_xor(place, block)]

    weight = weight_ref[...].reshape(depth, tile)
    term = jnp.dot(lhs_ref[...], weight, preferred_element_type=jnp.float32)
    both = term.astype(jnp.bfloat16).reshape(2, shards // 2, rows, tile)
    send_ref[...] = both[0]
    keep_ref[...] = both[1]


def project(place, rot, weight, order, first, width):
    shards, rows, depth = rot.shape
    groups, planes, words, _ = weight.shape
    tile = 1024
    start = first // tile
    full = tuple(q ^ 1 for q in order) + tuple(order)
    shape = jax.ShapeDtypeStruct((shards // 2, rows, width), jnp.bfloat16)
    return pl.pallas_call(
        functools.partial(project_body, full),
        grid_spec=pltpu.PrefetchScalarGridSpec(
            num_scalar_prefetch=1,
            grid=(width // tile,),
            in_specs=[
                pl.BlockSpec((shards, rows, depth), lambda j, p: (0, 0, 0)),
                pl.BlockSpec((groups, planes, words, tile), lambda j, p: (0, 0, 0, j + start)),
            ],
            out_specs=[
                pl.BlockSpec((shards // 2, rows, tile), lambda j, p: (0, 0, j)),
                pl.BlockSpec((shards // 2, rows, tile), lambda j, p: (0, 0, j)),
            ],
            scratch_shapes=[pltpu.VMEM((shards * rows, depth), jnp.bfloat16)],
        ),
        out_shape=[shape, shape],
        compiler_params=pltpu.CompilerParams(vmem_limit_bytes=VMEM_LIMIT),
        cost_estimate=pl.CostEstimate(
            flops=2 * shards * rows * depth * width,
            bytes_accessed=2 * depth * width + 4 * shards * rows * width,
            transcendentals=0,
        ),
        name="project",
    )(place, rot, weight)


def place_body(names, first, width, count, place_ref, *refs):
    pieces, out_ref, sems = refs[:count], refs[-2], refs[-1]
    rows = pieces[0].shape[1]
    copies = []
    for piece, blocks in zip(pieces, names):
        for at, block in enumerate(blocks):
            start = pl.multiple_of(jnp.bitwise_xor(place_ref[0], block) * rows, rows)
            copies.append(
                pltpu.make_async_copy(
                    piece.at[at],
                    out_ref.at[pl.ds(start, rows), pl.ds(first, width)],
                    sems.at[len(copies)],
                )
            )
    for copy in copies:
        copy.start()
    for copy in copies:
        copy.wait()


def put(place, pieces, names, first, shape, into=None):
    count = len(pieces)
    width = pieces[0].shape[2]
    extra = () if into is None else (into,)
    return pl.pallas_call(
        functools.partial(place_body, names, first, width, count),
        in_specs=[pl.BlockSpec(memory_space=pltpu.SMEM)]
        + [pl.BlockSpec(memory_space=pl.ANY)] * (count + len(extra)),
        out_specs=pl.BlockSpec(memory_space=pl.ANY),
        out_shape=jax.ShapeDtypeStruct(shape, jnp.bfloat16),
        scratch_shapes=[pltpu.SemaphoreType.DMA((sum(map(len, names)),))],
        input_output_aliases={} if into is None else {1 + count: 0},
        compiler_params=pltpu.CompilerParams(vmem_limit_bytes=VMEM_LIMIT),
        cost_estimate=pl.CostEstimate(
            flops=0, bytes_accessed=4 * sum(p.size for p in pieces), transcendentals=0
        ),
        name="put",
    )(place, *pieces, *extra)


def local(gate_input, up_input, down_low, down_high, down_scales):
    shards = lax.axis_size("tensor")
    total_rows, local_ff = gate_input.shape
    rows = total_rows // shards
    groups = local_ff // GROUP
    width = down_low.shape[1]
    half = width // 2
    place = lax.axis_index("tensor").astype(jnp.int32).reshape(1)
    f32, bf16 = jnp.float32, jnp.bfloat16

    def swap(x, mask):
        return lax.ppermute(x, "tensor", [(i, i ^ mask) for i in range(shards)])

    CORE, Y = 1, 8
    X = (0, 2, 4, 6)
    by_x = tuple(x | y for x in X for y in (0, Y))
    by_y = tuple(x | y for y in (0, Y) for x in X)

    hidden = (jax.nn.silu(gate_input.astype(f32)) * up_input.astype(f32)).astype(bf16)
    mine = lax.all_to_all(hidden.reshape(shards, rows, local_ff), "tensor", 0, 0)
    turned = rotate(mine, local_table(local_ff))
    rot = lax.all_to_all(turned, "tensor", 0, 0)

    weight = dequant(
        down_low.reshape(groups, GROUP // 8, width),
        down_high.reshape(groups, GROUP // 8, width),
        down_scales.reshape(groups, 1, width),
    )

    keep_p, send_p = project(place, rot, weight, by_x, 0, half)
    got_p = swap(send_p, CORE)
    keep_q, send_q = project(place, rot, weight, by_y, half, half)
    got_q = swap(send_q, CORE)

    def chip_p(k):
        at = slice(2 * k, 2 * k + 2)
        return keep_p[at].astype(f32) + got_p[at].astype(f32)

    def chip_q(y):
        at = slice(4 * y, 4 * y + 4)
        return keep_q[at].astype(f32) + got_q[at].astype(f32)

    along_x = [swap(chip_p(k).astype(bf16), X[k]) for k in (2, 1, 3)]
    along_y = swap(chip_q(1).astype(bf16), Y)
    sum_p = chip_p(0) + sum(t.astype(f32) for t in along_x)
    sum_q = chip_q(0) + along_y.astype(f32)
    last_p = swap(sum_p[1].astype(bf16), Y)
    last_q = [swap(sum_q[k].astype(bf16), X[k]) for k in (2, 1, 3)]
    done_p = (sum_p[0] + last_p.astype(f32)).astype(bf16)
    done_q = (sum_q[0] + sum(t.astype(f32) for t in last_q)).astype(bf16)

    pair_p = jnp.stack([done_p, swap(done_p, Y)])
    row_q = jnp.stack([done_q] + [swap(done_q, X[k]) for k in (1, 2, 3)])
    all_p = [pair_p] + [swap(pair_p, X[k]) for k in (1, 2, 3)]
    all_q = [row_q, swap(row_q, Y)]
    names_p = [tuple(X[k] | y for y in (0, Y)) for k in range(4)]
    names_q = [tuple(x | y for x in X) for y in (0, Y)]
    far_p = [swap(t, CORE) for t in all_p]
    far_q = [swap(t, CORE) for t in all_q]

    def across(names):
        return [tuple(q | CORE for q in blocks) for blocks in names]

    shape = (total_rows, width)
    out = put(place, all_p + far_p, names_p + across(names_p), 0, shape)
    return put(place, all_q + far_q, names_q + across(names_q), half, shape, out)


def solution(mesh):
    placed = (
        P("dp", "tensor"),
        P("dp", "tensor"),
        P("tensor", None),
        P("tensor", None),
        P("tensor", None),
    )
    return jax.shard_map(local, mesh=mesh, in_specs=placed, out_specs=P("dp", None), check_vma=False)
```

```python
import functools
import math

import jax
import jax.numpy as jnp
import numpy as np
from jax import lax
from jax.experimental import pallas as pl
from jax.experimental.pallas import tpu as pltpu
from jax.sharding import PartitionSpec as P

FF = 26624
GROUP = 128
CODE_FLIP = 0x8888
VMEM_LIMIT = 32 * 1024 * 1024


def paley_table():
    elements = [(u, v) for v in range(5) for u in range(5)]
    squares = set()
    for u, v in elements:
        if u != 0 or v != 0:
            squares.add(((u * u + 2 * v * v) % 5, 2 * u * v % 5))
    quad = np.zeros((25, 25))
    for i, first in enumerate(elements):
        for j, second in enumerate(elements):
            diff = ((first[0] - second[0]) % 5, (first[1] - second[1]) % 5)
            if diff != (0, 0):
                quad[i, j] = 1.0 if diff in squares else -1.0
    core = np.zeros((26, 26))
    core[0, 1:] = 1.0
    core[1:, 0] = 1.0
    core[1:, 1:] = quad
    return np.kron(core, np.array([[1.0, 1.0], [1.0, -1.0]])) + np.kron(
        np.eye(26), np.array([[1.0, -1.0], [-1.0, -1.0]])
    )


def sylvester(order):
    table = np.ones((1, 1))
    while table.shape[0] < order:
        table = np.kron(np.array([[1.0, 1.0], [1.0, -1.0]]), table)
    return table


def local_table(local_ff):
    table = np.kron(sylvester(local_ff // 52), paley_table())
    order = np.arange(local_ff).reshape(-1, GROUP // 8, 8).transpose(0, 2, 1).reshape(-1)
    tile = 512
    table = np.pad(table[:, order], ((0, 0), (0, -local_ff % tile)))
    return jnp.asarray(table.reshape(local_ff, -1, tile).transpose(1, 0, 2), jnp.bfloat16)


def in_hbm(x):
    return pltpu.with_memory_space_constraint(x, pltpu.HBM)


def rotate_body(hidden_ref, table_ref, out_ref, table_buf, sems):
    shards, rows, depth = hidden_ref.shape
    tiles, _, tile = table_buf.shape
    copies = [pltpu.make_async_copy(table_ref.at[j], table_buf.at[j], sems.at[j]) for j in range(tiles)]
    for copy in copies:
        copy.start()
    flat = hidden_ref[...].reshape(shards * rows, depth)
    for j in range(tiles):
        copies[j].wait()
        turned = jnp.dot(flat, table_buf[j], preferred_element_type=jnp.float32)
        parts = [turned[rows * s : rows * (s + 1)] for s in range(shards)]
        step = 1
        while step < shards:
            parts = [
                parts[s] + parts[s + step] if s & step == 0 else parts[s - step] - parts[s]
                for s in range(shards)
            ]
            step *= 2
        used = min(tile, depth - tile * j)
        for s in range(shards):
            scaled = (parts[s] * (1.0 / math.sqrt(FF))).astype(jnp.bfloat16)
            out_ref[s, :, tile * j : tile * j + used] = scaled[:, :used]


def rotate(hidden, table):
    shards, rows, depth = hidden.shape
    return pl.pallas_call(
        rotate_body,
        in_specs=[pl.BlockSpec(memory_space=pltpu.VMEM), pl.BlockSpec(memory_space=pltpu.HBM)],
        out_specs=pl.BlockSpec(memory_space=pltpu.VMEM),
        out_shape=jax.ShapeDtypeStruct(hidden.shape, jnp.bfloat16),
        scratch_shapes=[
            pltpu.VMEM(table.shape, jnp.bfloat16),
            pltpu.SemaphoreType.DMA((table.shape[0],)),
        ],
        compiler_params=pltpu.CompilerParams(vmem_limit_bytes=VMEM_LIMIT),
        cost_estimate=pl.CostEstimate(
            flops=2 * shards * rows * depth * depth,
            bytes_accessed=2 * depth * depth + 4 * shards * rows * depth,
            transcendentals=0,
        ),
        name="rotate",
    )(hidden, in_hbm(table))


def unpack(low_ref, high_ref, scale_ref, first, out_ref):
    depth, tile = out_ref.shape
    words = GROUP // 8
    cols = slice(first, first + tile)
    for g in range(depth // GROUP):
        scale = jnp.broadcast_to(scale_ref[g : g + 1, cols].astype(jnp.float32), (words, tile))
        for half, ref in enumerate((low_ref, high_ref)):
            nibbles = (ref[words * g : words * (g + 1), cols] + 34952) ^ CODE_FLIP
            for k in range(4):
                code = (nibbles << (28 - 4 * k)) >> 28
                row = GROUP * g + words * (4 * half + k)
                out_ref[row : row + words] = (code.astype(jnp.float32) * scale).astype(jnp.bfloat16)


def project_body(order, place_ref, rot_ref, low_ref, high_ref, scale_ref, keep_ref, send_ref, lhs_ref, weight_ref):
    shards, rows, depth = rot_ref.shape
    tile = weight_ref.shape[1]

    @pl.when(pl.program_id(0) == 0)
    def _():
        for at, block in enumerate(order):
            lhs_ref[rows * at : rows * (at + 1)] = rot_ref[jnp.bitwise_xor(place_ref[0], block)]

    for first in range(0, keep_ref.shape[2], tile):
        unpack(low_ref, high_ref, scale_ref, first, weight_ref)
        term = jnp.dot(lhs_ref[...], weight_ref[...], preferred_element_type=jnp.float32)
        both = term.astype(jnp.bfloat16).reshape(2, shards // 2, rows, tile)
        send_ref[:, :, first : first + tile] = both[0]
        keep_ref[:, :, first : first + tile] = both[1]


def project(place, rot, low, high, scales, order, first, width):
    shards, rows, depth = rot.shape
    tile = 512
    step = 2 * tile
    start = first // step
    full = tuple(q ^ 1 for q in order) + tuple(order)
    shape = jax.ShapeDtypeStruct((shards // 2, rows, width), jnp.bfloat16)

    def columns(j, p):
        return (0, start + j)

    return pl.pallas_call(
        functools.partial(project_body, full),
        grid_spec=pltpu.PrefetchScalarGridSpec(
            num_scalar_prefetch=1,
            grid=(width // step,),
            in_specs=[
                pl.BlockSpec((shards, rows, depth), lambda j, p: (0, 0, 0)),
                pl.BlockSpec((low.shape[0], step), columns),
                pl.BlockSpec((high.shape[0], step), columns),
                pl.BlockSpec((scales.shape[0], step), columns),
            ],
            out_specs=[pl.BlockSpec((shards // 2, rows, step), lambda j, p: (0, 0, j))] * 2,
            scratch_shapes=[
                pltpu.VMEM((shards * rows, depth), jnp.bfloat16),
                pltpu.VMEM((depth, tile), jnp.bfloat16),
            ],
        ),
        out_shape=[shape, shape],
        compiler_params=pltpu.CompilerParams(vmem_limit_bytes=VMEM_LIMIT),
        cost_estimate=pl.CostEstimate(
            flops=2 * shards * rows * depth * width,
            bytes_accessed=depth * width + 4 * shards * rows * width,
            transcendentals=0,
        ),
        name="project",
    )(place, rot, in_hbm(low), in_hbm(high), in_hbm(scales))


def put_body(names, firsts, place_ref, *refs):
    pieces, out_ref, sems = refs[:-2], refs[-2], refs[-1]
    copies = []
    for piece, blocks, first in zip(pieces, names, firsts):
        _, rows, width = piece.shape
        for at, block in enumerate(blocks):
            start = pl.multiple_of(jnp.bitwise_xor(place_ref[0], block) * rows, rows)
            copies.append(
                pltpu.make_async_copy(
                    piece.at[at],
                    out_ref.at[pl.ds(start, rows), pl.ds(first, width)],
                    sems.at[len(copies)],
                )
            )
    for copy in copies:
        copy.start()
    for copy in copies:
        copy.wait()


def put(place, pieces, names, firsts, shape):
    return pl.pallas_call(
        functools.partial(put_body, names, firsts),
        in_specs=[pl.BlockSpec(memory_space=pltpu.SMEM)] + [pl.BlockSpec(memory_space=pl.ANY)] * len(pieces),
        out_specs=pl.BlockSpec(memory_space=pl.ANY),
        out_shape=jax.ShapeDtypeStruct(shape, jnp.bfloat16),
        scratch_shapes=[pltpu.SemaphoreType.DMA((sum(map(len, names)),))],
        compiler_params=pltpu.CompilerParams(vmem_limit_bytes=VMEM_LIMIT),
        cost_estimate=pl.CostEstimate(
            flops=0, bytes_accessed=4 * sum(p.size for p in pieces), transcendentals=0
        ),
        name="put",
    )(place, *pieces)


def local(gate_input, up_input, down_low, down_high, down_scales):
    shards = lax.axis_size("tensor")
    total_rows, local_ff = gate_input.shape
    rows = total_rows // shards
    width = down_low.shape[1]
    left = width // 8 * 5
    place = lax.axis_index("tensor").astype(jnp.int32).reshape(1)
    f32, bf16 = jnp.float32, jnp.bfloat16

    def swap(x, mask):
        return lax.ppermute(x, "tensor", [(i, i ^ mask) for i in range(shards)])

    CORE, Y = 1, 8
    X = (0, 2, 4, 6)
    by_x = tuple(x | y for x in X for y in (0, Y))
    by_y = tuple(x | y for y in (0, Y) for x in X)

    hidden = (jax.nn.silu(gate_input.astype(f32)) * up_input.astype(f32)).astype(bf16)
    mine = lax.all_to_all(hidden.reshape(shards, rows, local_ff), "tensor", 0, 0)
    turned = rotate(mine, local_table(local_ff))
    rot = lax.all_to_all(turned, "tensor", 0, 0)
    codes = (down_low, down_high, down_scales)

    keep_p, send_p = project(place, rot, *codes, by_x, 0, left)
    got_p = swap(send_p, CORE)
    keep_q, send_q = project(place, rot, *codes, by_y, left, width - left)
    got_q = swap(send_q, CORE)

    def chip_p(k):
        at = slice(2 * k, 2 * k + 2)
        return keep_p[at].astype(f32) + got_p[at].astype(f32)

    def chip_q(y):
        at = slice(4 * y, 4 * y + 4)
        return keep_q[at].astype(f32) + got_q[at].astype(f32)

    along_x = [swap(chip_p(k).astype(bf16), X[k]) for k in (2, 1, 3)]
    along_y = swap(chip_q(1).astype(bf16), Y)
    sum_p = chip_p(0) + sum(t.astype(f32) for t in along_x)
    sum_q = chip_q(0) + along_y.astype(f32)

    mine_p = lax.reduce_precision(sum_p, 8, 7)
    theirs_p = swap(mine_p.astype(bf16), Y)
    last_q = [swap(sum_q[k].astype(bf16), X[k]) for k in (2, 1, 3)]
    done_p = (mine_p + theirs_p[::-1].astype(f32)).astype(bf16)
    done_q = (sum_q[0] + sum(t.astype(f32) for t in last_q)).astype(bf16)

    all_p = [done_p] + [swap(done_p, X[k]) for k in (2, 1, 3)]
    row_q = jnp.stack([done_q] + [swap(done_q, X[k]) for k in (1, 2, 3)])
    all_q = [row_q, swap(row_q, Y)]
    names_p = [tuple(X[k] | y for y in (0, Y)) for k in (0, 2, 1, 3)]
    names_q = [tuple(x | y for x in X) for y in (0, Y)]
    near = all_p + all_q
    names = names_p + names_q
    far = [swap(t, CORE) for t in near]
    names += [tuple(q | CORE for q in blocks) for blocks in names]
    firsts = [0] * len(all_p) + [left] * len(all_q)
    return put(place, near + far, names, firsts * 2, (total_rows, width))


def solution(mesh):
    placed = (
        P("dp", "tensor"),
        P("dp", "tensor"),
        P("tensor", None),
        P("tensor", None),
        P("tensor", None),
    )
    return jax.shard_map(local, mesh=mesh, in_specs=placed, out_specs=P("dp", None), check_vma=False)
```

```python
import functools
import math

import jax
import jax.numpy as jnp
import numpy as np
from jax import lax
from jax.experimental import pallas as pl
from jax.experimental.pallas import tpu as pltpu
from jax.sharding import PartitionSpec as P

FF = 26624
GROUP = 128
CODE_FLIP = 0x8888
VMEM_LIMIT = 32 * 1024 * 1024


def paley_table():
    elements = [(u, v) for v in range(5) for u in range(5)]
    squares = set()
    for u, v in elements:
        if u != 0 or v != 0:
            squares.add(((u * u + 2 * v * v) % 5, 2 * u * v % 5))
    quad = np.zeros((25, 25))
    for i, first in enumerate(elements):
        for j, second in enumerate(elements):
            diff = ((first[0] - second[0]) % 5, (first[1] - second[1]) % 5)
            if diff != (0, 0):
                quad[i, j] = 1.0 if diff in squares else -1.0
    core = np.zeros((26, 26))
    core[0, 1:] = 1.0
    core[1:, 0] = 1.0
    core[1:, 1:] = quad
    return np.kron(core, np.array([[1.0, 1.0], [1.0, -1.0]])) + np.kron(
        np.eye(26), np.array([[1.0, -1.0], [-1.0, -1.0]])
    )


def sylvester(order):
    table = np.ones((1, 1))
    while table.shape[0] < order:
        table = np.kron(np.array([[1.0, 1.0], [1.0, -1.0]]), table)
    return table


def local_table(local_ff):
    table = np.kron(sylvester(local_ff // 52), paley_table())
    order = np.arange(local_ff).reshape(-1, GROUP // 8, 8).transpose(0, 2, 1).reshape(-1)
    tile = 512
    table = np.pad(table[:, order], ((0, 0), (0, -local_ff % tile)))
    return jnp.asarray(table.reshape(local_ff, -1, tile).transpose(1, 0, 2), jnp.bfloat16)


def in_hbm(x):
    return pltpu.with_memory_space_constraint(x, pltpu.HBM)


def rotate_body(hidden_ref, table_ref, out_ref, table_buf, sems):
    shards, rows, depth = hidden_ref.shape
    tiles, _, tile = table_buf.shape
    copies = [pltpu.make_async_copy(table_ref.at[j], table_buf.at[j], sems.at[j]) for j in range(tiles)]
    for copy in copies:
        copy.start()
    flat = hidden_ref[...].reshape(shards * rows, depth)
    for j in range(tiles):
        copies[j].wait()
        turned = jnp.dot(flat, table_buf[j], preferred_element_type=jnp.float32)
        parts = [turned[rows * s : rows * (s + 1)] for s in range(shards)]
        step = 1
        while step < shards:
            parts = [
                parts[s] + parts[s + step] if s & step == 0 else parts[s - step] - parts[s]
                for s in range(shards)
            ]
            step *= 2
        used = min(tile, depth - tile * j)
        for s in range(shards):
            scaled = (parts[s] * (1.0 / math.sqrt(FF))).astype(jnp.bfloat16)
            out_ref[s, :, tile * j : tile * j + used] = scaled[:, :used]


def rotate(hidden, table):
    shards, rows, depth = hidden.shape
    return pl.pallas_call(
        rotate_body,
        in_specs=[pl.BlockSpec(memory_space=pltpu.VMEM), pl.BlockSpec(memory_space=pltpu.HBM)],
        out_specs=pl.BlockSpec(memory_space=pltpu.VMEM),
        out_shape=jax.ShapeDtypeStruct(hidden.shape, jnp.bfloat16),
        scratch_shapes=[
            pltpu.VMEM(table.shape, jnp.bfloat16),
            pltpu.SemaphoreType.DMA((table.shape[0],)),
        ],
        compiler_params=pltpu.CompilerParams(vmem_limit_bytes=VMEM_LIMIT),
        cost_estimate=pl.CostEstimate(
            flops=2 * shards * rows * depth * depth,
            bytes_accessed=2 * depth * depth + 4 * shards * rows * depth,
            transcendentals=0,
        ),
        name="rotate",
    )(hidden, in_hbm(table))


def unpack(low_ref, high_ref, scale_ref, first, out_ref):
    depth, tile = out_ref.shape
    words = GROUP // 8
    cols = slice(first, first + tile)
    for g in range(depth // GROUP):
        scale = jnp.broadcast_to(scale_ref[g : g + 1, cols].astype(jnp.float32), (words, tile))
        for half, ref in enumerate((low_ref, high_ref)):
            nibbles = (ref[words * g : words * (g + 1), cols] + 34952) ^ CODE_FLIP
            for k in range(4):
                code = (nibbles << (28 - 4 * k)) >> 28
                row = GROUP * g + words * (4 * half + k)
                out_ref[row : row + words] = (code.astype(jnp.float32) * scale).astype(jnp.bfloat16)


def project_body(order, place_ref, rot_ref, low_ref, high_ref, scale_ref, keep_ref, send_ref, lhs_ref, weight_ref):
    shards, rows, depth = rot_ref.shape
    tile = weight_ref.shape[1]

    @pl.when(pl.program_id(0) == 0)
    def _():
        for at, block in enumerate(order):
            lhs_ref[rows * at : rows * (at + 1)] = rot_ref[jnp.bitwise_xor(place_ref[0], block)]

    for first in range(0, keep_ref.shape[2], tile):
        unpack(low_ref, high_ref, scale_ref, first, weight_ref)
        term = jnp.dot(lhs_ref[...], weight_ref[...], preferred_element_type=jnp.float32)
        both = term.astype(jnp.bfloat16).reshape(2, shards // 2, rows, tile)
        send_ref[:, :, first : first + tile] = both[0]
        keep_ref[:, :, first : first + tile] = both[1]


def project(place, rot, low, high, scales, order, first, width):
    shards, rows, depth = rot.shape
    tile = 512
    step = 2 * tile
    start = first // step
    full = tuple(q ^ 1 for q in order) + tuple(order)
    shape = jax.ShapeDtypeStruct((shards // 2, rows, width), jnp.bfloat16)

    def columns(j, p):
        return (0, start + j)

    return pl.pallas_call(
        functools.partial(project_body, full),
        grid_spec=pltpu.PrefetchScalarGridSpec(
            num_scalar_prefetch=1,
            grid=(width // step,),
            in_specs=[
                pl.BlockSpec((shards, rows, depth), lambda j, p: (0, 0, 0)),
                pl.BlockSpec((low.shape[0], step), columns),
                pl.BlockSpec((high.shape[0], step), columns),
                pl.BlockSpec((scales.shape[0], step), columns),
            ],
            out_specs=[pl.BlockSpec((shards // 2, rows, step), lambda j, p: (0, 0, j))] * 2,
            scratch_shapes=[
                pltpu.VMEM((shards * rows, depth), jnp.bfloat16),
                pltpu.VMEM((depth, tile), jnp.bfloat16),
            ],
        ),
        out_shape=[shape, shape],
        compiler_params=pltpu.CompilerParams(vmem_limit_bytes=VMEM_LIMIT),
        cost_estimate=pl.CostEstimate(
            flops=2 * shards * rows * depth * width,
            bytes_accessed=depth * width + 4 * shards * rows * width,
            transcendentals=0,
        ),
        name="project",
    )(place, rot, in_hbm(low), in_hbm(high), in_hbm(scales))


def put_body(names, firsts, place_ref, *refs):
    pieces, out_ref, sems = refs[:-2], refs[-2], refs[-1]
    copies = []
    for piece, blocks, first in zip(pieces, names, firsts):
        _, rows, width = piece.shape
        for at, block in enumerate(blocks):
            start = pl.multiple_of(jnp.bitwise_xor(place_ref[0], block) * rows, rows)
            copies.append(
                pltpu.make_async_copy(
                    piece.at[at],
                    out_ref.at[pl.ds(start, rows), pl.ds(first, width)],
                    sems.at[len(copies)],
                )
            )
    for copy in copies:
        copy.start()
    for copy in copies:
        copy.wait()


def put(place, pieces, names, firsts, shape, into=None, weight=0):
    extra = () if into is None else (into,)
    return pl.pallas_call(
        functools.partial(put_body, names, firsts),
        in_specs=[pl.BlockSpec(memory_space=pltpu.SMEM)]
        + [pl.BlockSpec(memory_space=pl.ANY)] * (len(pieces) + len(extra)),
        out_specs=pl.BlockSpec(memory_space=pl.ANY),
        out_shape=jax.ShapeDtypeStruct(shape, jnp.bfloat16),
        scratch_shapes=[pltpu.SemaphoreType.DMA((sum(map(len, names)),))],
        input_output_aliases={} if into is None else {1 + len(pieces): 0},
        compiler_params=pltpu.CompilerParams(vmem_limit_bytes=VMEM_LIMIT),
        cost_estimate=pl.CostEstimate(
            flops=weight, bytes_accessed=4 * sum(p.size for p in pieces), transcendentals=0
        ),
        name="put",
    )(place, *pieces, *extra)


def local(gate_input, up_input, down_low, down_high, down_scales):
    shards = lax.axis_size("tensor")
    total_rows, local_ff = gate_input.shape
    rows = total_rows // shards
    width = down_low.shape[1]
    left = width // 8 * 4
    place = lax.axis_index("tensor").astype(jnp.int32).reshape(1)
    f32, bf16 = jnp.float32, jnp.bfloat16

    def swap(x, mask):
        return lax.ppermute(x, "tensor", [(i, i ^ mask) for i in range(shards)])

    CORE, Y = 1, 8
    X = (0, 2, 4, 6)
    by_x = tuple(x | y for x in X for y in (0, Y))
    by_y = tuple(x | y for y in (0, Y) for x in X)

    hidden = (jax.nn.silu(gate_input.astype(f32)) * up_input.astype(f32)).astype(bf16)
    mine = lax.all_to_all(hidden.reshape(shards, rows, local_ff), "tensor", 0, 0)
    turned = rotate(mine, local_table(local_ff))
    rot = lax.all_to_all(turned, "tensor", 0, 0)
    codes = (down_low, down_high, down_scales)

    keep_p, send_p = project(place, rot, *codes, by_x, 0, left)
    got_p = swap(send_p, CORE)
    keep_q, send_q = project(place, rot, *codes, by_y, left, width - left)
    got_q = swap(send_q, CORE)

    def chip_p(k):
        at = slice(2 * k, 2 * k + 2)
        return keep_p[at].astype(f32) + got_p[at].astype(f32)

    def chip_q(y):
        at = slice(4 * y, 4 * y + 4)
        return keep_q[at].astype(f32) + got_q[at].astype(f32)

    sends_p = [chip_p(k).astype(bf16) for k in (2, 1, 3)]
    along_x = [swap(t, X[k]) for t, k in zip(sends_p, (2, 1, 3))]
    along_y = swap(chip_q(1).astype(bf16), Y)
    sum_p = chip_p(0) + sum(t.astype(f32) for t in along_x)
    along_y, *_ = lax.optimization_barrier((along_y, *sends_p))
    sum_q = chip_q(0) + along_y.astype(f32)

    mine_p = lax.reduce_precision(sum_p, 8, 7)
    theirs_p = swap(mine_p.astype(bf16), Y)
    last_q = [swap(sum_q[k].astype(bf16), X[k]) for k in (2, 1, 3)]
    done_p = (mine_p + theirs_p[::-1].astype(f32)).astype(bf16)
    done_q = (sum_q[0] + sum(t.astype(f32) for t in last_q)).astype(bf16)

    all_p = [done_p] + [swap(done_p, X[k]) for k in (2, 1, 3)]
    row_q = [done_q] + [swap(done_q, X[k]) for k in (1, 2, 3)]
    *row_q, _ = lax.optimization_barrier((*row_q, done_p))
    row_q = jnp.stack(row_q)
    all_q = [row_q, swap(row_q, Y)]
    names_p = [tuple(X[k] | y for y in (0, Y)) for k in (0, 2, 1, 3)]
    names_q = [tuple(x | y for x in X) for y in (0, Y)]
    far_p = [swap(t, CORE) for t in all_p]
    far_q = [swap(t, CORE) for t in all_q]

    def across(names):
        return [tuple(q | CORE for q in blocks) for blocks in names]

    def lay(into, pieces, names, first, weight):
        return put(place, pieces, names, [first] * len(pieces), (total_rows, width), into, weight)

    out = lay(None, all_p[:1], names_p[:1], 0, 20000000000)
    out = lay(out, all_q + far_q, names_q + across(names_q), left, 0)
    out = lay(out, all_p[1:] + far_p[:1], names_p[1:] + across(names_p[:1]), 0, 20000000000)
    return lay(out, far_p[1:], across(names_p[1:]), 0, 0)


def solution(mesh):
    placed = (
        P("dp", "tensor"),
        P("dp", "tensor"),
        P("tensor", None),
        P("tensor", None),
        P("tensor", None),
    )
    return jax.shard_map(local, mesh=mesh, in_specs=placed, out_specs=P("dp", None), check_vma=False)
```

```python
import functools
import math

import jax
import jax.numpy as jnp
import numpy as np
from jax import lax
from jax.experimental import pallas as pl
from jax.experimental.pallas import tpu as pltpu
from jax.sharding import PartitionSpec as P

FF = 26624
GROUP = 128
CODE_FLIP = 0x8888
VMEM_LIMIT = 32 * 1024 * 1024


def paley_table():
    elements = [(u, v) for v in range(5) for u in range(5)]
    squares = set()
    for u, v in elements:
        if u != 0 or v != 0:
            squares.add(((u * u + 2 * v * v) % 5, 2 * u * v % 5))
    quad = np.zeros((25, 25))
    for i, first in enumerate(elements):
        for j, second in enumerate(elements):
            diff = ((first[0] - second[0]) % 5, (first[1] - second[1]) % 5)
            if diff != (0, 0):
                quad[i, j] = 1.0 if diff in squares else -1.0
    core = np.zeros((26, 26))
    core[0, 1:] = 1.0
    core[1:, 0] = 1.0
    core[1:, 1:] = quad
    return np.kron(core, np.array([[1.0, 1.0], [1.0, -1.0]])) + np.kron(
        np.eye(26), np.array([[1.0, -1.0], [-1.0, -1.0]])
    )


def sylvester(order):
    table = np.ones((1, 1))
    while table.shape[0] < order:
        table = np.kron(np.array([[1.0, 1.0], [1.0, -1.0]]), table)
    return table


def local_table(local_ff):
    table = np.kron(sylvester(local_ff // 52), paley_table())
    order = np.arange(local_ff).reshape(-1, GROUP // 8, 8).transpose(0, 2, 1).reshape(-1)
    tile = 512
    table = np.pad(table[:, order], ((0, 0), (0, -local_ff % tile)))
    return jnp.asarray(table.reshape(local_ff, -1, tile).transpose(1, 0, 2), jnp.bfloat16)


def in_hbm(x):
    return pltpu.with_memory_space_constraint(x, pltpu.HBM)


def rotate_body(hidden_ref, table_ref, out_ref, table_buf, sems):
    shards, rows, depth = hidden_ref.shape
    tiles, _, tile = table_buf.shape
    copies = [pltpu.make_async_copy(table_ref.at[j], table_buf.at[j], sems.at[j]) for j in range(tiles)]
    for copy in copies:
        copy.start()
    flat = hidden_ref[...].reshape(shards * rows, depth)
    for j in range(tiles):
        copies[j].wait()
        turned = jnp.dot(flat, table_buf[j], preferred_element_type=jnp.float32)
        parts = [turned[rows * s : rows * (s + 1)] for s in range(shards)]
        step = 1
        while step < shards:
            parts = [
                parts[s] + parts[s + step] if s & step == 0 else parts[s - step] - parts[s]
                for s in range(shards)
            ]
            step *= 2
        used = min(tile, depth - tile * j)
        for s in range(shards):
            scaled = (parts[s] * (1.0 / math.sqrt(FF))).astype(jnp.bfloat16)
            out_ref[s, :, tile * j : tile * j + used] = scaled[:, :used]


def rotate(hidden, table):
    shards, rows, depth = hidden.shape
    return pl.pallas_call(
        rotate_body,
        in_specs=[pl.BlockSpec(memory_space=pltpu.VMEM), pl.BlockSpec(memory_space=pltpu.HBM)],
        out_specs=pl.BlockSpec(memory_space=pltpu.VMEM),
        out_shape=jax.ShapeDtypeStruct(hidden.shape, jnp.bfloat16),
        scratch_shapes=[
            pltpu.VMEM(table.shape, jnp.bfloat16),
            pltpu.SemaphoreType.DMA((table.shape[0],)),
        ],
        compiler_params=pltpu.CompilerParams(vmem_limit_bytes=VMEM_LIMIT),
        cost_estimate=pl.CostEstimate(
            flops=2 * shards * rows * depth * depth,
            bytes_accessed=2 * depth * depth + 4 * shards * rows * depth,
            transcendentals=0,
        ),
        name="rotate",
    )(hidden, in_hbm(table))


def unpack(low_ref, high_ref, scale_ref, first, out_ref):
    depth, tile = out_ref.shape
    words = GROUP // 8
    cols = slice(first, first + tile)
    for g in range(depth // GROUP):
        scale = jnp.broadcast_to(scale_ref[g : g + 1, cols].astype(jnp.float32), (words, tile))
        for half, ref in enumerate((low_ref, high_ref)):
            nibbles = (ref[words * g : words * (g + 1), cols] + 34952) ^ CODE_FLIP
            for k in range(4):
                code = (nibbles << (28 - 4 * k)) >> 28
                row = GROUP * g + words * (4 * half + k)
                out_ref[row : row + words] = (code.astype(jnp.float32) * scale).astype(jnp.bfloat16)


def project_body(order, place_ref, rot_ref, low_ref, high_ref, scale_ref, keep_ref, send_ref, lhs_ref, weight_ref):
    shards, rows, depth = rot_ref.shape
    tile = weight_ref.shape[1]

    @pl.when(pl.program_id(0) == 0)
    def _():
        for at, block in enumerate(order):
            lhs_ref[rows * at : rows * (at + 1)] = rot_ref[jnp.bitwise_xor(place_ref[0], block)]

    for first in range(0, keep_ref.shape[2], tile):
        unpack(low_ref, high_ref, scale_ref, first, weight_ref)
        term = jnp.dot(lhs_ref[...], weight_ref[...], preferred_element_type=jnp.float32)
        both = term.astype(jnp.bfloat16).reshape(2, shards // 2, rows, tile)
        send_ref[:, :, first : first + tile] = both[0]
        keep_ref[:, :, first : first + tile] = both[1]


def project(place, rot, low, high, scales, order, first, width):
    shards, rows, depth = rot.shape
    tile = 512
    step = 2 * tile
    start = first // step
    full = tuple(q ^ 1 for q in order) + tuple(order)
    shape = jax.ShapeDtypeStruct((shards // 2, rows, width), jnp.bfloat16)

    def columns(j, p):
        return (0, start + j)

    return pl.pallas_call(
        functools.partial(project_body, full),
        grid_spec=pltpu.PrefetchScalarGridSpec(
            num_scalar_prefetch=1,
            grid=(width // step,),
            in_specs=[
                pl.BlockSpec((shards, rows, depth), lambda j, p: (0, 0, 0)),
                pl.BlockSpec((low.shape[0], step), columns),
                pl.BlockSpec((high.shape[0], step), columns),
                pl.BlockSpec((scales.shape[0], step), columns),
            ],
            out_specs=[pl.BlockSpec((shards // 2, rows, step), lambda j, p: (0, 0, j))] * 2,
            scratch_shapes=[
                pltpu.VMEM((shards * rows, depth), jnp.bfloat16),
                pltpu.VMEM((depth, tile), jnp.bfloat16),
            ],
        ),
        out_shape=[shape, shape],
        compiler_params=pltpu.CompilerParams(vmem_limit_bytes=VMEM_LIMIT),
        cost_estimate=pl.CostEstimate(
            flops=2 * shards * rows * depth * width,
            bytes_accessed=depth * width + 4 * shards * rows * width,
            transcendentals=0,
        ),
        name="project",
    )(place, rot, in_hbm(low), in_hbm(high), in_hbm(scales))


TILE = 1024
CUTS = 4


def dequant_body(low_ref, high_ref, scale_ref, out_ref, buf, sems):
    step, steps = pl.program_id(0), pl.num_programs(0)
    depth = buf.shape[1]

    def stores(at):
        slot = at % 2
        cuts = [pl.ds(depth // CUTS * i, depth // CUTS) for i in range(CUTS)]
        return [pltpu.make_async_copy(buf.at[slot, c], out_ref.at[at, c], sems.at[slot, i]) for i, c in enumerate(cuts)]

    @pl.when(step >= 2)
    def _():
        for copy in stores(step - 2):
            copy.wait()

    unpack(low_ref, high_ref, scale_ref, 0, buf.at[step % 2])
    for copy in stores(step):
        copy.start()

    @pl.when(step == steps - 1)
    def _():
        for at in (steps - 2, steps - 1):
            for copy in stores(at):
                copy.wait()


def dequant(low, high, scales, first, width):
    depth = low.shape[0] * 8
    tiles, start = width // TILE, first // TILE
    return pl.pallas_call(
        dequant_body,
        grid=(tiles,),
        in_specs=[
            pl.BlockSpec((low.shape[0], TILE), lambda j: (0, j + start)),
            pl.BlockSpec((high.shape[0], TILE), lambda j: (0, j + start)),
            pl.BlockSpec((scales.shape[0], TILE), lambda j: (0, j + start)),
        ],
        out_specs=pl.BlockSpec(memory_space=pltpu.HBM),
        out_shape=pltpu.HBM((tiles, depth, TILE), jnp.bfloat16),
        scratch_shapes=[pltpu.VMEM((2, depth, TILE), jnp.bfloat16), pltpu.SemaphoreType.DMA((2, CUTS))],
        compiler_params=pltpu.CompilerParams(vmem_limit_bytes=VMEM_LIMIT),
        cost_estimate=pl.CostEstimate(
            flops=8 * depth * width,
            bytes_accessed=3 * depth * width,
            transcendentals=0,
        ),
        name="dequant",
    )(in_hbm(low), in_hbm(high), in_hbm(scales))


def stream_body(order, place_ref, rot_ref, weight_ref, keep_ref, send_ref, lhs_ref, buf, sems):
    shards, rows, depth = rot_ref.shape
    step, steps = pl.program_id(0), pl.num_programs(0)
    slots = buf.shape[0]

    def loads(at):
        slot = at % slots
        cuts = [pl.ds(depth // CUTS * i, depth // CUTS) for i in range(CUTS)]
        return [pltpu.make_async_copy(weight_ref.at[at, c], buf.at[slot, c], sems.at[slot, i]) for i, c in enumerate(cuts)]

    def load(at):
        @pl.when(at < steps)
        def _():
            for copy in loads(at):
                copy.start()

    @pl.when(step == 0)
    def _():
        load(0)
        load(1)
        for at, block in enumerate(order):
            lhs_ref[rows * at : rows * (at + 1)] = rot_ref[jnp.bitwise_xor(place_ref[0], block)]

    load(step + 2)
    for copy in loads(step):
        copy.wait()
    term = jnp.dot(lhs_ref[...], buf[step % slots], preferred_element_type=jnp.float32)
    both = term.astype(jnp.bfloat16).reshape(2, shards // 2, rows, TILE)
    send_ref[...] = both[0]
    keep_ref[...] = both[1]


def project_unpacked(place, rot, weights, order):
    shards, rows, depth = rot.shape
    tiles = weights.shape[0]
    full = tuple(q ^ 1 for q in order) + tuple(order)
    shape = jax.ShapeDtypeStruct((shards // 2, rows, tiles * TILE), jnp.bfloat16)
    return pl.pallas_call(
        functools.partial(stream_body, full),
        grid_spec=pltpu.PrefetchScalarGridSpec(
            num_scalar_prefetch=1,
            grid=(tiles,),
            in_specs=[
                pl.BlockSpec((shards, rows, depth), lambda j, p: (0, 0, 0)),
                pl.BlockSpec(memory_space=pltpu.HBM),
            ],
            out_specs=[pl.BlockSpec((shards // 2, rows, TILE), lambda j, p: (0, 0, j))] * 2,
            scratch_shapes=[
                pltpu.VMEM((shards * rows, depth), jnp.bfloat16),
                pltpu.VMEM((3, depth, TILE), jnp.bfloat16),
                pltpu.SemaphoreType.DMA((3, CUTS)),
            ],
        ),
        out_shape=[shape, shape],
        compiler_params=pltpu.CompilerParams(vmem_limit_bytes=VMEM_LIMIT),
        cost_estimate=pl.CostEstimate(
            flops=2 * shards * rows * depth * tiles * TILE,
            bytes_accessed=2 * depth * tiles * TILE + 4 * shards * rows * tiles * TILE,
            transcendentals=0,
        ),
        name="project_unpacked",
    )(place, rot, in_hbm(weights))


def put_body(names, firsts, place_ref, *refs):
    pieces, out_ref, sems = refs[:-2], refs[-2], refs[-1]
    copies = []
    for piece, blocks, first in zip(pieces, names, firsts):
        _, rows, width = piece.shape
        for at, block in enumerate(blocks):
            start = pl.multiple_of(jnp.bitwise_xor(place_ref[0], block) * rows, rows)
            copies.append(
                pltpu.make_async_copy(
                    piece.at[at],
                    out_ref.at[pl.ds(start, rows), pl.ds(first, width)],
                    sems.at[len(copies)],
                )
            )
    for copy in copies:
        copy.start()
    for copy in copies:
        copy.wait()


def put(place, pieces, names, firsts, shape, into=None, weight=0):
    extra = () if into is None else (into,)
    return pl.pallas_call(
        functools.partial(put_body, names, firsts),
        in_specs=[pl.BlockSpec(memory_space=pltpu.SMEM)]
        + [pl.BlockSpec(memory_space=pl.ANY)] * (len(pieces) + len(extra)),
        out_specs=pl.BlockSpec(memory_space=pl.ANY),
        out_shape=jax.ShapeDtypeStruct(shape, jnp.bfloat16),
        scratch_shapes=[pltpu.SemaphoreType.DMA((sum(map(len, names)),))],
        input_output_aliases={} if into is None else {1 + len(pieces): 0},
        compiler_params=pltpu.CompilerParams(vmem_limit_bytes=VMEM_LIMIT),
        cost_estimate=pl.CostEstimate(
            flops=weight, bytes_accessed=4 * sum(p.size for p in pieces), transcendentals=0
        ),
        name="put",
    )(place, *pieces, *extra)


def local(gate_input, up_input, down_low, down_high, down_scales):
    shards = lax.axis_size("tensor")
    total_rows, local_ff = gate_input.shape
    rows = total_rows // shards
    width = down_low.shape[1]
    left = width // 8 * 4
    place = lax.axis_index("tensor").astype(jnp.int32).reshape(1)
    f32, bf16 = jnp.float32, jnp.bfloat16

    def swap(x, mask):
        return lax.ppermute(x, "tensor", [(i, i ^ mask) for i in range(shards)])

    CORE, Y = 1, 8
    X = (0, 2, 4, 6)
    by_x = tuple(x | y for x in X for y in (0, Y))
    by_y = tuple(x | y for y in (0, Y) for x in X)

    hidden = (jax.nn.silu(gate_input.astype(f32)) * up_input.astype(f32)).astype(bf16)
    mine = lax.all_to_all(hidden.reshape(shards, rows, local_ff), "tensor", 0, 0)
    turned = rotate(mine, local_table(local_ff))
    rot = lax.all_to_all(turned, "tensor", 0, 0)
    codes = (down_low, down_high, down_scales)
    weights = dequant(*codes, left, width - left)
    rot, weights = lax.optimization_barrier((rot, weights))

    keep_p, send_p = project(place, rot, *codes, by_x, 0, left)
    got_p = swap(send_p, CORE)
    keep_q, send_q = project_unpacked(place, rot, weights, by_y)
    got_q = swap(send_q, CORE)

    def chip_p(k):
        at = slice(2 * k, 2 * k + 2)
        return keep_p[at].astype(f32) + got_p[at].astype(f32)

    def chip_q(y):
        at = slice(4 * y, 4 * y + 4)
        return keep_q[at].astype(f32) + got_q[at].astype(f32)

    sends_p = [chip_p(k).astype(bf16) for k in (2, 1, 3)]
    along_x = [swap(t, X[k]) for t, k in zip(sends_p, (2, 1, 3))]
    along_y = swap(chip_q(1).astype(bf16), Y)
    sum_p = chip_p(0) + sum(t.astype(f32) for t in along_x)
    along_y, *_ = lax.optimization_barrier((along_y, *sends_p))
    sum_q = chip_q(0) + along_y.astype(f32)

    mine_p = lax.reduce_precision(sum_p, 8, 7)
    theirs_p = swap(mine_p.astype(bf16), Y)
    last_q = [swap(sum_q[k].astype(bf16), X[k]) for k in (2, 1, 3)]
    done_p = (mine_p + theirs_p[::-1].astype(f32)).astype(bf16)
    done_q = (sum_q[0] + sum(t.astype(f32) for t in last_q)).astype(bf16)

    all_p = [done_p] + [swap(done_p, X[k]) for k in (1, 3, 2)]
    row_q = [done_q] + [swap(done_q, X[k]) for k in (1, 2, 3)]
    *row_q, _ = lax.optimization_barrier((*row_q, done_p))
    row_q = jnp.stack(row_q)
    all_q = [row_q, swap(row_q, Y)]
    names_p = [tuple(X[k] | y for y in (0, Y)) for k in (0, 1, 3, 2)]
    names_q = [tuple(x | y for x in X) for y in (0, Y)]
    far_p = [swap(t, CORE) for t in all_p]
    far_q = [swap(t, CORE) for t in all_q]

    def across(names):
        return [tuple(q | CORE for q in blocks) for blocks in names]

    def lay(into, pieces, names, first, weight):
        return put(place, pieces, names, [first] * len(pieces), (total_rows, width), into, weight)

    out = lay(None, all_p[:1], names_p[:1], 0, 20000000000)
    out = lay(out, all_p[1:] + far_p[:1], names_p[1:] + across(names_p[:1]), 0, 20000000000)
    out = lay(out, all_q + far_q, names_q + across(names_q), left, 0)
    return lay(out, far_p[1:], across(names_p[1:]), 0, 0)


def solution(mesh):
    placed = (
        P("dp", "tensor"),
        P("dp", "tensor"),
        P("tensor", None),
        P("tensor", None),
        P("tensor", None),
    )
    return jax.shard_map(local, mesh=mesh, in_specs=placed, out_specs=P("dp", None), check_vma=False)
```

```python
import functools
import math

import jax
import jax.numpy as jnp
import numpy as np
from jax import lax
from jax.experimental import pallas as pl
from jax.experimental.pallas import tpu as pltpu
from jax.sharding import PartitionSpec as P

FF = 26624
GROUP = 128
CODE_FLIP = 0x8888
VMEM_LIMIT = 32 * 1024 * 1024


def paley_table():
    elements = [(u, v) for v in range(5) for u in range(5)]
    squares = set()
    for u, v in elements:
        if u != 0 or v != 0:
            squares.add(((u * u + 2 * v * v) % 5, 2 * u * v % 5))
    quad = np.zeros((25, 25))
    for i, first in enumerate(elements):
        for j, second in enumerate(elements):
            diff = ((first[0] - second[0]) % 5, (first[1] - second[1]) % 5)
            if diff != (0, 0):
                quad[i, j] = 1.0 if diff in squares else -1.0
    core = np.zeros((26, 26))
    core[0, 1:] = 1.0
    core[1:, 0] = 1.0
    core[1:, 1:] = quad
    return np.kron(core, np.array([[1.0, 1.0], [1.0, -1.0]])) + np.kron(
        np.eye(26), np.array([[1.0, -1.0], [-1.0, -1.0]])
    )


def sylvester(order):
    table = np.ones((1, 1))
    while table.shape[0] < order:
        table = np.kron(np.array([[1.0, 1.0], [1.0, -1.0]]), table)
    return table


def local_table(local_ff):
    table = np.kron(sylvester(local_ff // 52), paley_table())
    order = np.arange(local_ff).reshape(-1, GROUP // 8, 8).transpose(0, 2, 1).reshape(-1)
    tile = 512
    table = np.pad(table[:, order], ((0, 0), (0, -local_ff % tile)))
    return jnp.asarray(table.reshape(local_ff, -1, tile).transpose(1, 0, 2), jnp.bfloat16)


def in_hbm(x):
    return pltpu.with_memory_space_constraint(x, pltpu.HBM)


def rotate_body(hidden_ref, table_ref, out_ref, table_buf, sems):
    shards, rows, depth = hidden_ref.shape
    tiles, _, tile = table_buf.shape
    copies = [pltpu.make_async_copy(table_ref.at[j], table_buf.at[j], sems.at[j]) for j in range(tiles)]
    for copy in copies:
        copy.start()
    flat = hidden_ref[...].reshape(shards * rows, depth)
    for j in range(tiles):
        copies[j].wait()
        turned = jnp.dot(flat, table_buf[j], preferred_element_type=jnp.float32)
        parts = [turned[rows * s : rows * (s + 1)] for s in range(shards)]
        step = 1
        while step < shards:
            parts = [
                parts[s] + parts[s + step] if s & step == 0 else parts[s - step] - parts[s]
                for s in range(shards)
            ]
            step *= 2
        used = min(tile, depth - tile * j)
        for s in range(shards):
            scaled = (parts[s] * (1.0 / math.sqrt(FF))).astype(jnp.bfloat16)
            out_ref[s, :, tile * j : tile * j + used] = scaled[:, :used]


def rotate(hidden, table):
    shards, rows, depth = hidden.shape
    return pl.pallas_call(
        rotate_body,
        in_specs=[pl.BlockSpec(memory_space=pltpu.VMEM), pl.BlockSpec(memory_space=pltpu.HBM)],
        out_specs=pl.BlockSpec(memory_space=pltpu.VMEM),
        out_shape=jax.ShapeDtypeStruct(hidden.shape, jnp.bfloat16),
        scratch_shapes=[
            pltpu.VMEM(table.shape, jnp.bfloat16),
            pltpu.SemaphoreType.DMA((table.shape[0],)),
        ],
        compiler_params=pltpu.CompilerParams(vmem_limit_bytes=VMEM_LIMIT),
        cost_estimate=pl.CostEstimate(
            flops=2 * shards * rows * depth * depth,
            bytes_accessed=2 * depth * depth + 4 * shards * rows * depth,
            transcendentals=0,
        ),
        name="rotate",
    )(hidden, in_hbm(table))


def unpack(low_ref, high_ref, scale_ref, first, out_ref):
    depth, tile = out_ref.shape
    words = GROUP // 8
    cols = slice(first, first + tile)
    for g in range(depth // GROUP):
        scale = jnp.broadcast_to(scale_ref[g : g + 1, cols].astype(jnp.float32), (words, tile))
        for half, ref in enumerate((low_ref, high_ref)):
            nibbles = (ref[words * g : words * (g + 1), cols] + 34952) ^ CODE_FLIP
            for k in range(4):
                code = (nibbles << (28 - 4 * k)) >> 28
                row = GROUP * g + words * (4 * half + k)
                out_ref[row : row + words] = (code.astype(jnp.float32) * scale).astype(jnp.bfloat16)


def project_body(order, place_ref, rot_ref, low_ref, high_ref, scale_ref, keep_ref, send_ref, lhs_ref, weight_ref):
    shards, rows, depth = rot_ref.shape
    tile = weight_ref.shape[1]

    @pl.when(pl.program_id(0) == 0)
    def _():
        for at, block in enumerate(order):
            lhs_ref[rows * at : rows * (at + 1)] = rot_ref[jnp.bitwise_xor(place_ref[0], block)]

    for first in range(0, keep_ref.shape[2], tile):
        unpack(low_ref, high_ref, scale_ref, first, weight_ref)
        term = jnp.dot(lhs_ref[...], weight_ref[...], preferred_element_type=jnp.float32)
        both = term.astype(jnp.bfloat16).reshape(2, shards // 2, rows, tile)
        send_ref[:, :, first : first + tile] = both[0]
        keep_ref[:, :, first : first + tile] = both[1]


def project(place, rot, low, high, scales, order, first, width):
    shards, rows, depth = rot.shape
    tile = 512
    step = 2 * tile
    start = first // step
    full = tuple(q ^ 1 for q in order) + tuple(order)
    shape = jax.ShapeDtypeStruct((shards // 2, rows, width), jnp.bfloat16)

    def columns(j, p):
        return (0, start + j)

    return pl.pallas_call(
        functools.partial(project_body, full),
        grid_spec=pltpu.PrefetchScalarGridSpec(
            num_scalar_prefetch=1,
            grid=(width // step,),
            in_specs=[
                pl.BlockSpec((shards, rows, depth), lambda j, p: (0, 0, 0)),
                pl.BlockSpec((low.shape[0], step), columns),
                pl.BlockSpec((high.shape[0], step), columns),
                pl.BlockSpec((scales.shape[0], step), columns),
            ],
            out_specs=[pl.BlockSpec((shards // 2, rows, step), lambda j, p: (0, 0, j))] * 2,
            scratch_shapes=[
                pltpu.VMEM((shards * rows, depth), jnp.bfloat16),
                pltpu.VMEM((depth, tile), jnp.bfloat16),
            ],
        ),
        out_shape=[shape, shape],
        compiler_params=pltpu.CompilerParams(vmem_limit_bytes=VMEM_LIMIT),
        cost_estimate=pl.CostEstimate(
            flops=2 * shards * rows * depth * width,
            bytes_accessed=depth * width + 4 * shards * rows * width,
            transcendentals=0,
        ),
        name="project",
    )(place, rot, in_hbm(low), in_hbm(high), in_hbm(scales))


TILE = 1024
CUTS = 4


def dequant_body(low_ref, high_ref, scale_ref, out_ref, buf, sems):
    step, steps = pl.program_id(0), pl.num_programs(0)
    depth = buf.shape[1]

    def stores(at):
        slot = at % 2
        cuts = [pl.ds(depth // CUTS * i, depth // CUTS) for i in range(CUTS)]
        return [pltpu.make_async_copy(buf.at[slot, c], out_ref.at[at, c], sems.at[slot, i]) for i, c in enumerate(cuts)]

    @pl.when(step >= 2)
    def _():
        for copy in stores(step - 2):
            copy.wait()

    unpack(low_ref, high_ref, scale_ref, 0, buf.at[step % 2])
    for copy in stores(step):
        copy.start()

    @pl.when(step == steps - 1)
    def _():
        for at in (steps - 2, steps - 1):
            for copy in stores(at):
                copy.wait()


def dequant(low, high, scales, first, width):
    depth = low.shape[0] * 8
    tiles, start = width // TILE, first // TILE
    return pl.pallas_call(
        dequant_body,
        grid=(tiles,),
        in_specs=[
            pl.BlockSpec((low.shape[0], TILE), lambda j: (0, j + start)),
            pl.BlockSpec((high.shape[0], TILE), lambda j: (0, j + start)),
            pl.BlockSpec((scales.shape[0], TILE), lambda j: (0, j + start)),
        ],
        out_specs=pl.BlockSpec(memory_space=pltpu.HBM),
        out_shape=pltpu.HBM((tiles, depth, TILE), jnp.bfloat16),
        scratch_shapes=[pltpu.VMEM((2, depth, TILE), jnp.bfloat16), pltpu.SemaphoreType.DMA((2, CUTS))],
        compiler_params=pltpu.CompilerParams(vmem_limit_bytes=VMEM_LIMIT),
        cost_estimate=pl.CostEstimate(
            flops=8 * depth * width,
            bytes_accessed=3 * depth * width,
            transcendentals=0,
        ),
        name="dequant",
    )(in_hbm(low), in_hbm(high), in_hbm(scales))


def stream_body(order, place_ref, rot_ref, weight_ref, keep_ref, send_ref, lhs_ref, buf, sems):
    shards, rows, depth = rot_ref.shape
    step, steps = pl.program_id(0), pl.num_programs(0)
    slots = buf.shape[0]

    def loads(at):
        slot = at % slots
        cuts = [pl.ds(depth // CUTS * i, depth // CUTS) for i in range(CUTS)]
        return [pltpu.make_async_copy(weight_ref.at[at, c], buf.at[slot, c], sems.at[slot, i]) for i, c in enumerate(cuts)]

    def load(at):
        @pl.when(at < steps)
        def _():
            for copy in loads(at):
                copy.start()

    @pl.when(step == 0)
    def _():
        load(0)
        load(1)
        for at, block in enumerate(order):
            lhs_ref[rows * at : rows * (at + 1)] = rot_ref[jnp.bitwise_xor(place_ref[0], block)]

    load(step + 2)
    for copy in loads(step):
        copy.wait()
    term = jnp.dot(lhs_ref[...], buf[step % slots], preferred_element_type=jnp.float32)
    both = term.astype(jnp.bfloat16).reshape(2, shards // 2, rows, TILE)
    send_ref[...] = both[0]
    keep_ref[...] = both[1]


def project_unpacked(place, rot, weights, order):
    shards, rows, depth = rot.shape
    tiles = weights.shape[0]
    full = tuple(q ^ 1 for q in order) + tuple(order)
    shape = jax.ShapeDtypeStruct((shards // 2, rows, tiles * TILE), jnp.bfloat16)
    return pl.pallas_call(
        functools.partial(stream_body, full),
        grid_spec=pltpu.PrefetchScalarGridSpec(
            num_scalar_prefetch=1,
            grid=(tiles,),
            in_specs=[
                pl.BlockSpec((shards, rows, depth), lambda j, p: (0, 0, 0)),
                pl.BlockSpec(memory_space=pltpu.HBM),
            ],
            out_specs=[pl.BlockSpec((shards // 2, rows, TILE), lambda j, p: (0, 0, j))] * 2,
            scratch_shapes=[
                pltpu.VMEM((shards * rows, depth), jnp.bfloat16),
                pltpu.VMEM((3, depth, TILE), jnp.bfloat16),
                pltpu.SemaphoreType.DMA((3, CUTS)),
            ],
        ),
        out_shape=[shape, shape],
        compiler_params=pltpu.CompilerParams(vmem_limit_bytes=VMEM_LIMIT),
        cost_estimate=pl.CostEstimate(
            flops=2 * shards * rows * depth * tiles * TILE,
            bytes_accessed=2 * depth * tiles * TILE + 4 * shards * rows * tiles * TILE,
            transcendentals=0,
        ),
        name="project_unpacked",
    )(place, rot, in_hbm(weights))


def put_body(names, firsts, place_ref, *refs):
    pieces, out_ref, sems = refs[:-2], refs[-2], refs[-1]
    copies = []
    for piece, blocks, first in zip(pieces, names, firsts):
        _, rows, width = piece.shape
        for at, block in enumerate(blocks):
            start = pl.multiple_of(jnp.bitwise_xor(place_ref[0], block) * rows, rows)
            copies.append(
                pltpu.make_async_copy(
                    piece.at[at],
                    out_ref.at[pl.ds(start, rows), pl.ds(first, width)],
                    sems.at[len(copies)],
                )
            )
    for copy in copies:
        copy.start()
    for copy in copies:
        copy.wait()


def put(place, pieces, names, firsts, shape, into=None, weight=0):
    extra = () if into is None else (into,)
    return pl.pallas_call(
        functools.partial(put_body, names, firsts),
        in_specs=[pl.BlockSpec(memory_space=pltpu.SMEM)]
        + [pl.BlockSpec(memory_space=pl.ANY)] * (len(pieces) + len(extra)),
        out_specs=pl.BlockSpec(memory_space=pl.ANY),
        out_shape=jax.ShapeDtypeStruct(shape, jnp.bfloat16),
        scratch_shapes=[pltpu.SemaphoreType.DMA((sum(map(len, names)),))],
        input_output_aliases={} if into is None else {1 + len(pieces): 0},
        compiler_params=pltpu.CompilerParams(vmem_limit_bytes=VMEM_LIMIT),
        cost_estimate=pl.CostEstimate(
            flops=weight, bytes_accessed=4 * sum(p.size for p in pieces), transcendentals=0
        ),
        name="put",
    )(place, *pieces, *extra)


def local(gate_input, up_input, down_low, down_high, down_scales):
    shards = lax.axis_size("tensor")
    total_rows, local_ff = gate_input.shape
    rows = total_rows // shards
    width = down_low.shape[1]
    left = width // 8 * 4
    place = lax.axis_index("tensor").astype(jnp.int32).reshape(1)
    f32, bf16 = jnp.float32, jnp.bfloat16

    def swap(x, mask):
        return lax.ppermute(x, "tensor", [(i, i ^ mask) for i in range(shards)])

    CORE, Y = 1, 8
    X = (0, 2, 4, 6)
    by_x = tuple(x | y for x in X for y in (0, Y))
    by_y = tuple(x | y for y in (0, Y) for x in X)

    hidden = (jax.nn.silu(gate_input.astype(f32)) * up_input.astype(f32)).astype(bf16)
    mine = lax.all_to_all(hidden.reshape(shards, rows, local_ff), "tensor", 0, 0)
    turned = rotate(mine, local_table(local_ff))
    rot = lax.all_to_all(turned, "tensor", 0, 0)
    codes = (down_low, down_high, down_scales)
    weights = dequant(*codes, left, width - left)
    rot, weights = lax.optimization_barrier((rot, weights))

    keep_p, send_p = project(place, rot, *codes, by_x, 0, left)
    got_p = swap(send_p, CORE)
    keep_q, send_q = project_unpacked(place, rot, weights, by_y)
    got_q = swap(send_q, CORE)

    def chip_p(k):
        at = slice(2 * k, 2 * k + 2)
        return keep_p[at].astype(f32) + got_p[at].astype(f32)

    def chip_q(y):
        at = slice(4 * y, 4 * y + 4)
        return keep_q[at].astype(f32) + got_q[at].astype(f32)

    sends_p = [chip_p(k).astype(bf16) for k in (2, 1, 3)]
    along_x = [swap(t, X[k]) for t, k in zip(sends_p, (2, 1, 3))]
    along_y = swap(chip_q(1).astype(bf16), Y)
    sum_p = chip_p(0) + sum(t.astype(f32) for t in along_x)
    along_y, *_ = lax.optimization_barrier((along_y, *sends_p))
    sum_q = chip_q(0) + along_y.astype(f32)

    mine_p = lax.reduce_precision(sum_p, 8, 7)
    theirs_p = swap(mine_p.astype(bf16), Y)
    last_q = [swap(sum_q[k].astype(bf16), X[k]) for k in (2, 1, 3)]
    done_p = (mine_p + theirs_p[::-1].astype(f32)).astype(bf16)
    done_q = (sum_q[0] + sum(t.astype(f32) for t in last_q)).astype(bf16)

    all_p = [done_p] + [swap(done_p, X[k]) for k in (1, 3, 2)]
    row_q = [done_q] + [swap(done_q, X[k]) for k in (1, 2, 3)]
    *row_q, _ = lax.optimization_barrier((*row_q, done_p))
    row_q = jnp.stack(row_q)
    all_q = [row_q, swap(row_q, Y)]
    names_p = [tuple(X[k] | y for y in (0, Y)) for k in (0, 1, 3, 2)]
    names_q = [tuple(x | y for x in X) for y in (0, Y)]
    far_p = [swap(t, CORE) for t in all_p]
    far_q = [swap(t, CORE) for t in all_q]

    def across(names):
        return [tuple(q | CORE for q in blocks) for blocks in names]

    out = put(
        place,
        all_p[:1],
        names_p[:1],
        [0] * len(all_p[:1]),
        (total_rows, width),
        None,
        20000000000,
    )
    out = put(
        place,
        all_p[1:] + far_p[:1],
        names_p[1:] + across(names_p[:1]),
        [0] * len(all_p[1:]) + [0] * len(far_p[:1]),
        (total_rows, width),
        out,
        20000000000,
    )
    out = put(
        place,
        far_p[1:] + all_q[:1] + far_q[:1],
        across(names_p[1:]) + names_q[:1] + across(names_q[:1]),
        [0] * len(far_p[1:]) + [left] * len(all_q[:1]) + [left] * len(far_q[:1]),
        (total_rows, width),
        out,
        0,
    )
    out = put(
        place,
        all_q[1:] + far_q[1:],
        names_q[1:] + across(names_q[1:]),
        [left] * len(all_q[1:]) + [left] * len(far_q[1:]),
        (total_rows, width),
        out,
        0,
    )
    return out


def solution(mesh):
    placed = (
        P("dp", "tensor"),
        P("dp", "tensor"),
        P("tensor", None),
        P("tensor", None),
        P("tensor", None),
    )
    return jax.shard_map(local, mesh=mesh, in_specs=placed, out_specs=P("dp", None), check_vma=False)
```

```python
import functools
import math

import jax
import jax.numpy as jnp
import numpy as np
from jax import lax
from jax.experimental import pallas as pl
from jax.experimental.pallas import tpu as pltpu
from jax.sharding import PartitionSpec as P

FF = 26624
GROUP = 128
CODE_FLIP = 0x8888
VMEM_LIMIT = 32 * 1024 * 1024


def paley_table():
    elements = [(u, v) for v in range(5) for u in range(5)]
    squares = set()
    for u, v in elements:
        if u != 0 or v != 0:
            squares.add(((u * u + 2 * v * v) % 5, 2 * u * v % 5))
    quad = np.zeros((25, 25))
    for i, first in enumerate(elements):
        for j, second in enumerate(elements):
            diff = ((first[0] - second[0]) % 5, (first[1] - second[1]) % 5)
            if diff != (0, 0):
                quad[i, j] = 1.0 if diff in squares else -1.0
    core = np.zeros((26, 26))
    core[0, 1:] = 1.0
    core[1:, 0] = 1.0
    core[1:, 1:] = quad
    return np.kron(core, np.array([[1.0, 1.0], [1.0, -1.0]])) + np.kron(
        np.eye(26), np.array([[1.0, -1.0], [-1.0, -1.0]])
    )


def sylvester(order):
    table = np.ones((1, 1))
    while table.shape[0] < order:
        table = np.kron(np.array([[1.0, 1.0], [1.0, -1.0]]), table)
    return table


def local_table(local_ff):
    table = np.kron(sylvester(local_ff // 52), paley_table())
    order = np.arange(local_ff).reshape(-1, GROUP // 8, 8).transpose(0, 2, 1).reshape(-1)
    tile = 896
    table = np.pad(table[:, order], ((0, 0), (0, -local_ff % tile)))
    return jnp.asarray(table.reshape(local_ff, -1, tile).transpose(1, 0, 2), jnp.bfloat16)


def in_hbm(x):
    return pltpu.with_memory_space_constraint(x, pltpu.HBM)


def rotate_body(hidden_ref, table_ref, out_ref, table_buf, sems):
    shards, rows, depth = hidden_ref.shape
    tiles, _, tile = table_buf.shape
    copies = [pltpu.make_async_copy(table_ref.at[j], table_buf.at[j], sems.at[j]) for j in range(tiles)]
    for copy in copies:
        copy.start()
    flat = hidden_ref[...].reshape(shards * rows, depth)
    for j in range(tiles):
        copies[j].wait()
        turned = jnp.dot(flat, table_buf[j], preferred_element_type=jnp.float32)
        parts = [turned[rows * s : rows * (s + 1)] for s in range(shards)]
        step = 1
        while step < shards:
            parts = [
                parts[s] + parts[s + step] if s & step == 0 else parts[s - step] - parts[s]
                for s in range(shards)
            ]
            step *= 2
        used = min(tile, depth - tile * j)
        for s in range(shards):
            scaled = (parts[s] * (1.0 / math.sqrt(FF))).astype(jnp.bfloat16)
            out_ref[s, :, tile * j : tile * j + used] = scaled[:, :used]


def rotate(hidden, table):
    shards, rows, depth = hidden.shape
    return pl.pallas_call(
        rotate_body,
        in_specs=[pl.BlockSpec(memory_space=pltpu.VMEM), pl.BlockSpec(memory_space=pltpu.HBM)],
        out_specs=pl.BlockSpec(memory_space=pltpu.VMEM),
        out_shape=jax.ShapeDtypeStruct(hidden.shape, jnp.bfloat16),
        scratch_shapes=[
            pltpu.VMEM(table.shape, jnp.bfloat16),
            pltpu.SemaphoreType.DMA((table.shape[0],)),
        ],
        compiler_params=pltpu.CompilerParams(vmem_limit_bytes=VMEM_LIMIT),
        cost_estimate=pl.CostEstimate(
            flops=2 * shards * rows * depth * depth,
            bytes_accessed=2 * depth * depth + 4 * shards * rows * depth,
            transcendentals=0,
        ),
        name="rotate",
    )(hidden, in_hbm(table))


def unpack(low_ref, high_ref, scale_ref, first, out_ref):
    depth, tile = out_ref.shape
    words = GROUP // 8
    cols = slice(first, first + tile)
    for g in range(depth // GROUP):
        scale = jnp.broadcast_to(scale_ref[g : g + 1, cols].astype(jnp.float32), (words, tile))
        for half, ref in enumerate((low_ref, high_ref)):
            nibbles = (ref[words * g : words * (g + 1), cols] + 34952) ^ CODE_FLIP
            for k in range(4):
                code = (nibbles << (28 - 4 * k)) >> 28
                row = GROUP * g + words * (4 * half + k)
                out_ref[row : row + words] = (code.astype(jnp.float32) * scale).astype(jnp.bfloat16)


def project_body(order, place_ref, rot_ref, low_ref, high_ref, scale_ref, keep_ref, send_ref, lhs_ref, weight_ref):
    shards, rows, depth = rot_ref.shape
    tile = weight_ref.shape[1]

    @pl.when(pl.program_id(0) == 0)
    def _():
        for at, block in enumerate(order):
            lhs_ref[rows * at : rows * (at + 1)] = rot_ref[jnp.bitwise_xor(place_ref[0], block)]

    for first in range(0, keep_ref.shape[2], tile):
        unpack(low_ref, high_ref, scale_ref, first, weight_ref)
        term = jnp.dot(lhs_ref[...], weight_ref[...], preferred_element_type=jnp.float32)
        both = term.astype(jnp.bfloat16).reshape(2, shards // 2, rows, tile)
        send_ref[:, :, first : first + tile] = both[0]
        keep_ref[:, :, first : first + tile] = both[1]


def project(place, rot, low, high, scales, order, first, width):
    shards, rows, depth = rot.shape
    tile = 512
    step = 2 * tile
    start = first // step
    full = tuple(q ^ 1 for q in order) + tuple(order)
    shape = jax.ShapeDtypeStruct((shards // 2, rows, width), jnp.bfloat16)

    def columns(j, p):
        return (0, start + j)

    return pl.pallas_call(
        functools.partial(project_body, full),
        grid_spec=pltpu.PrefetchScalarGridSpec(
            num_scalar_prefetch=1,
            grid=(width // step,),
            in_specs=[
                pl.BlockSpec((shards, rows, depth), lambda j, p: (0, 0, 0)),
                pl.BlockSpec((low.shape[0], step), columns),
                pl.BlockSpec((high.shape[0], step), columns),
                pl.BlockSpec((scales.shape[0], step), columns),
            ],
            out_specs=[pl.BlockSpec((shards // 2, rows, step), lambda j, p: (0, 0, j))] * 2,
            scratch_shapes=[
                pltpu.VMEM((shards * rows, depth), jnp.bfloat16),
                pltpu.VMEM((depth, tile), jnp.bfloat16),
            ],
        ),
        out_shape=[shape, shape],
        compiler_params=pltpu.CompilerParams(vmem_limit_bytes=VMEM_LIMIT),
        cost_estimate=pl.CostEstimate(
            flops=2 * shards * rows * depth * width,
            bytes_accessed=depth * width + 4 * shards * rows * width,
            transcendentals=0,
        ),
        name="project",
    )(place, rot, in_hbm(low), in_hbm(high), in_hbm(scales))


TILE = 1024
CUTS = 4


def dequant_body(low_ref, high_ref, scale_ref, out_ref, buf, sems):
    step, steps = pl.program_id(0), pl.num_programs(0)
    depth = buf.shape[1]

    def stores(at):
        slot = at % 2
        cuts = [pl.ds(depth // CUTS * i, depth // CUTS) for i in range(CUTS)]
        return [pltpu.make_async_copy(buf.at[slot, c], out_ref.at[at, c], sems.at[slot, i]) for i, c in enumerate(cuts)]

    @pl.when(step >= 2)
    def _():
        for copy in stores(step - 2):
            copy.wait()

    unpack(low_ref, high_ref, scale_ref, 0, buf.at[step % 2])
    for copy in stores(step):
        copy.start()

    @pl.when(step == steps - 1)
    def _():
        for at in (steps - 2, steps - 1):
            for copy in stores(at):
                copy.wait()


def dequant(low, high, scales, first, width):
    depth = low.shape[0] * 8
    tiles, start = width // TILE, first // TILE
    return pl.pallas_call(
        dequant_body,
        grid=(tiles,),
        in_specs=[
            pl.BlockSpec((low.shape[0], TILE), lambda j: (0, j + start)),
            pl.BlockSpec((high.shape[0], TILE), lambda j: (0, j + start)),
            pl.BlockSpec((scales.shape[0], TILE), lambda j: (0, j + start)),
        ],
        out_specs=pl.BlockSpec(memory_space=pltpu.HBM),
        out_shape=pltpu.HBM((tiles, depth, TILE), jnp.bfloat16),
        scratch_shapes=[pltpu.VMEM((2, depth, TILE), jnp.bfloat16), pltpu.SemaphoreType.DMA((2, CUTS))],
        compiler_params=pltpu.CompilerParams(vmem_limit_bytes=VMEM_LIMIT),
        cost_estimate=pl.CostEstimate(
            flops=8 * depth * width,
            bytes_accessed=3 * depth * width,
            transcendentals=0,
        ),
        name="dequant",
    )(in_hbm(low), in_hbm(high), in_hbm(scales))


def stream_body(order, place_ref, rot_ref, weight_ref, keep_ref, send_ref, lhs_ref, buf, sems):
    shards, rows, depth = rot_ref.shape
    step, steps = pl.program_id(0), pl.num_programs(0)
    slots = buf.shape[0]

    def loads(at):
        slot = at % slots
        cuts = [pl.ds(depth // CUTS * i, depth // CUTS) for i in range(CUTS)]
        return [pltpu.make_async_copy(weight_ref.at[at, c], buf.at[slot, c], sems.at[slot, i]) for i, c in enumerate(cuts)]

    def load(at):
        @pl.when(at < steps)
        def _():
            for copy in loads(at):
                copy.start()

    @pl.when(step == 0)
    def _():
        load(0)
        load(1)
        for at, block in enumerate(order):
            lhs_ref[rows * at : rows * (at + 1)] = rot_ref[jnp.bitwise_xor(place_ref[0], block)]

    load(step + 2)
    for copy in loads(step):
        copy.wait()
    term = jnp.dot(lhs_ref[...], buf[step % slots], preferred_element_type=jnp.float32)
    both = term.astype(jnp.bfloat16).reshape(2, shards // 2, rows, TILE)
    send_ref[...] = both[0]
    keep_ref[...] = both[1]


def project_unpacked(place, rot, weights, order):
    shards, rows, depth = rot.shape
    tiles = weights.shape[0]
    full = tuple(q ^ 1 for q in order) + tuple(order)
    shape = jax.ShapeDtypeStruct((shards // 2, rows, tiles * TILE), jnp.bfloat16)
    return pl.pallas_call(
        functools.partial(stream_body, full),
        grid_spec=pltpu.PrefetchScalarGridSpec(
            num_scalar_prefetch=1,
            grid=(tiles,),
            in_specs=[
                pl.BlockSpec((shards, rows, depth), lambda j, p: (0, 0, 0)),
                pl.BlockSpec(memory_space=pltpu.HBM),
            ],
            out_specs=[pl.BlockSpec((shards // 2, rows, TILE), lambda j, p: (0, 0, j))] * 2,
            scratch_shapes=[
                pltpu.VMEM((shards * rows, depth), jnp.bfloat16),
                pltpu.VMEM((3, depth, TILE), jnp.bfloat16),
                pltpu.SemaphoreType.DMA((3, CUTS)),
            ],
        ),
        out_shape=[shape, shape],
        compiler_params=pltpu.CompilerParams(vmem_limit_bytes=VMEM_LIMIT),
        cost_estimate=pl.CostEstimate(
            flops=2 * shards * rows * depth * tiles * TILE,
            bytes_accessed=2 * depth * tiles * TILE + 4 * shards * rows * tiles * TILE,
            transcendentals=0,
        ),
        name="project_unpacked",
    )(place, rot, in_hbm(weights))


def put_body(names, firsts, place_ref, *refs):
    pieces, out_ref, sems = refs[:-2], refs[-2], refs[-1]
    copies = []
    for piece, blocks, first in zip(pieces, names, firsts):
        _, rows, width = piece.shape
        for at, block in enumerate(blocks):
            start = pl.multiple_of(jnp.bitwise_xor(place_ref[0], block) * rows, rows)
            copies.append(
                pltpu.make_async_copy(
                    piece.at[at],
                    out_ref.at[pl.ds(start, rows), pl.ds(first, width)],
                    sems.at[len(copies)],
                )
            )
    for copy in copies:
        copy.start()
    for copy in copies:
        copy.wait()


def put(place, pieces, names, firsts, shape, into=None, weight=0):
    extra = () if into is None else (into,)
    return pl.pallas_call(
        functools.partial(put_body, names, firsts),
        in_specs=[pl.BlockSpec(memory_space=pltpu.SMEM)]
        + [pl.BlockSpec(memory_space=pl.ANY)] * (len(pieces) + len(extra)),
        out_specs=pl.BlockSpec(memory_space=pl.ANY),
        out_shape=jax.ShapeDtypeStruct(shape, jnp.bfloat16),
        scratch_shapes=[pltpu.SemaphoreType.DMA((sum(map(len, names)),))],
        input_output_aliases={} if into is None else {1 + len(pieces): 0},
        compiler_params=pltpu.CompilerParams(vmem_limit_bytes=VMEM_LIMIT),
        cost_estimate=pl.CostEstimate(
            flops=weight, bytes_accessed=4 * sum(p.size for p in pieces), transcendentals=0
        ),
        name="put",
    )(place, *pieces, *extra)


def local(gate_input, up_input, down_low, down_high, down_scales):
    shards = lax.axis_size("tensor")
    total_rows, local_ff = gate_input.shape
    rows = total_rows // shards
    width = down_low.shape[1]
    left = width // 8 * 4
    place = lax.axis_index("tensor").astype(jnp.int32).reshape(1)
    f32, bf16 = jnp.float32, jnp.bfloat16

    def swap(x, mask):
        return lax.ppermute(x, "tensor", [(i, i ^ mask) for i in range(shards)])

    CORE, Y = 1, 8
    X = (0, 2, 4, 6)
    by_x = tuple(x | y for x in X for y in (0, Y))
    by_y = tuple(x | y for y in (0, Y) for x in X)

    hidden = (jax.nn.silu(gate_input.astype(f32)) * up_input.astype(f32)).astype(bf16)
    mine = lax.all_to_all(hidden.reshape(shards, rows, local_ff), "tensor", 0, 0)
    turned = rotate(mine, local_table(local_ff))
    rot = lax.all_to_all(turned, "tensor", 0, 0)
    codes = (down_low, down_high, down_scales)
    weights = dequant(*codes, left, width - left)
    rot, weights = lax.optimization_barrier((rot, weights))

    keep_p, send_p = project(place, rot, *codes, by_x, 0, left)
    got_p = swap(send_p, CORE)
    keep_q, send_q = project_unpacked(place, rot, weights, by_y)
    got_q = swap(send_q, CORE)

    def chip_p(k):
        at = slice(2 * k, 2 * k + 2)
        return keep_p[at].astype(f32) + got_p[at].astype(f32)

    def chip_q(y):
        at = slice(4 * y, 4 * y + 4)
        return keep_q[at].astype(f32) + got_q[at].astype(f32)

    sends_p = [chip_p(k).astype(bf16) for k in (2, 1, 3)]
    along_x = [swap(t, X[k]) for t, k in zip(sends_p, (2, 1, 3))]
    along_y = swap(chip_q(1).astype(bf16), Y)
    sum_p = chip_p(0) + sum(t.astype(f32) for t in along_x)
    along_y, *_ = lax.optimization_barrier((along_y, *sends_p))
    sum_q = chip_q(0) + along_y.astype(f32)

    mine_p = lax.reduce_precision(sum_p, 8, 7)
    theirs_p = swap(mine_p.astype(bf16), Y)
    last_q = [swap(sum_q[k].astype(bf16), X[k]) for k in (2, 1, 3)]
    done_p = (mine_p + theirs_p[::-1].astype(f32)).astype(bf16)
    done_q = (sum_q[0] + sum(t.astype(f32) for t in last_q)).astype(bf16)

    all_p = [done_p] + [swap(done_p, X[k]) for k in (1, 3, 2)]
    row_q = [done_q] + [swap(done_q, X[k]) for k in (1, 2, 3)]
    *row_q, _ = lax.optimization_barrier((*row_q, done_p))
    row_q = jnp.stack(row_q)
    all_q = [row_q, swap(row_q, Y)]
    names_p = [tuple(X[k] | y for y in (0, Y)) for k in (0, 1, 3, 2)]
    names_q = [tuple(x | y for x in X) for y in (0, Y)]
    far_p = [swap(t, CORE) for t in all_p]
    far_q = [swap(t, CORE) for t in all_q]

    def across(names):
        return [tuple(q | CORE for q in blocks) for blocks in names]

    out = put(
        place,
        all_p[:1],
        names_p[:1],
        [0] * len(all_p[:1]),
        (total_rows, width),
        None,
        20000000000,
    )
    out = put(
        place,
        all_p[1:] + far_p[:1],
        names_p[1:] + across(names_p[:1]),
        [0] * len(all_p[1:]) + [0] * len(far_p[:1]),
        (total_rows, width),
        out,
        20000000000,
    )
    out = put(
        place,
        far_p[1:] + all_q[:1] + far_q[:1],
        across(names_p[1:]) + names_q[:1] + across(names_q[:1]),
        [0] * len(far_p[1:]) + [left] * len(all_q[:1]) + [left] * len(far_q[:1]),
        (total_rows, width),
        out,
        0,
    )
    out = put(
        place,
        all_q[1:] + far_q[1:],
        names_q[1:] + across(names_q[1:]),
        [left] * len(all_q[1:]) + [left] * len(far_q[1:]),
        (total_rows, width),
        out,
        0,
    )
    return out


def solution(mesh):
    placed = (
        P("dp", "tensor"),
        P("dp", "tensor"),
        P("tensor", None),
        P("tensor", None),
        P("tensor", None),
    )
    return jax.shard_map(local, mesh=mesh, in_specs=placed, out_specs=P("dp", None), check_vma=False)
```
